256 devices in a mesh: tm: 8 (over z_lo, x), row: 4 (over z_hi), col: 8 (over y, core).
Axes of the slice: x: 4, y: 4, z: 8 (z_hi: 4, z_lo: 2; z = z_hi * 2 + z_lo), core: 2. Of those that a mesh axis runs over, the one named last changes fastest.
Arguments:
- matrix_tiles: float32 [32768, 16384], P(('tm', 'row'), 'col'), may hold values from -0.046875 to 0.046875
- block_map: int32 [128, 64], P(('tm', 'row'), 'col'), may hold values 0 or 1
- link_tiles: float32 [32768, 2048], P(('tm', 'row'), 'col'), may hold values from -0.125 to 0.125
- demand: float32 [32, 32768], P(None, ('tm', 'row')), may hold values from -6 to 6
- objective: float32 [131072], P(('tm', 'col')), may hold values from -6 to 6
- upper_bound: float32 [131072], P(('tm', 'col')), may hold values from 0.5 to 4
- restart_flag: int32 [3, 32], replicated, may hold values from 0 to 1
- step_index: int32 [3, 32], replicated, may hold values from 0 to 3
Outputs:
- primal: float32 [32, 131072], P(None, ('tm', 'col'))
- dual: float32 [32, 32768], P(None, ('tm', 'row'))
- kkt: float32 [8, 3, 32], P('tm')
The draws below stay inside these ranges and needn't reach their ends.
Inputs may be any that keep to these rules, and one draw needn't show every extreme that they name: `restart_flag`: 1 restarts that scenario's iterates from their averages after that iteration, 0 does not.
All inputs are finite; a program needn't handle non-finite values. No bound on the sum of `block_map` on one device may be relied on, other than what follows from the above.
Results may differ from the reference program's by a relative error of at most 0.0001.
Values sent between devices are 32-bit elements; how exact they have to be, the bound alone decides.
A program may use at most 128 MiB of HBM per device.

```python
import math
import jax
import jax.numpy as jnp
from jax import lax

COLS_DEV = 2048
STOR = 256
BLK = 256
S = 32
ITERS = 3
CON_T = 4096
VAR_T = 16384
NCON = 32768
NVAR = 131072
LINKW = 2048
N_TM = 8
N_COL = 8


def set_ends(values, rng, least, top_value):
    index_at = [jax.random.randint(jax.random.fold_in(rng, axis), (), 0, length) for axis, length in enumerate(values.shape)]
    main_axis = values.shape.index(max(values.shape))
    beside = index_at[:main_axis] + [(index_at[main_axis] + 1) % values.shape[main_axis]] + index_at[main_axis + 1:]
    return values.at[tuple(index_at)].set(least).at[tuple(beside)].set(top_value)


def levels(key, dims, shards, least, largest):
    def one(dim, shards_of):
        draws = jax.random.uniform(jax.random.fold_in(jax.random.fold_in(key, 6), dim), (shards_of,), jnp.float32, least / len(shards), largest / len(shards))
        return jnp.repeat(jnp.exp(draws), dims[dim] // shards_of).reshape((-1,) + (1,) * (len(dims) - dim - 1))

    loudness = one(*shards[0])
    for cut in shards[1:]:
        loudness = loudness * one(*cut)
    return loudness


def bell_draw(stream_key, shape, width, reach, cuts=(), held_as=jnp.bfloat16):
    entries = jax.random.normal(stream_key, shape, jnp.float32) * width
    if len(cuts) > 0:
        entries = levels(stream_key, shape, cuts, -0.22, 0.18) * entries
    return jnp.clip(entries, min=-reach, max=reach).astype(held_as)


def setup_inputs(seed: int = 0) -> dict:
    seeds = jax.random.split(jax.random.key(seed), 9)
    return {
        "matrix_tiles": bell_draw(seeds[0], (NCON, VAR_T), VAR_T ** -0.5, 0.046875, ((0, 32), (1, 8)), jnp.float32),
        "block_map": set_ends((jax.random.randint(seeds[1], (NCON // BLK, VAR_T // BLK), 0, 4) < 3).astype(jnp.int32), jax.random.fold_in(seeds[1], 1), 0, 1),
        "link_tiles": bell_draw(seeds[2], (NCON, LINKW), LINKW ** -0.5, 0.125, ((0, 32), (1, 8)), jnp.float32),
        "demand": bell_draw(seeds[3], (S, NCON), 1.0, 6.0, ((1, 32),), jnp.float32),
        "objective": bell_draw(seeds[4], (NVAR,), 1.0, 6.0, ((0, 64),), jnp.float32),
        "upper_bound": jnp.clip(jnp.exp(math.log(4.0) - 2.0794415 * jax.random.uniform(seeds[5], (NVAR,), jnp.float32) ** levels(seeds[5], (NVAR,), ((0, 64),), -0.2, 0.2)), 0.5, 4.0),
        "restart_flag": set_ends(jax.random.randint(seeds[6], (ITERS, S), 0, 2), jax.random.fold_in(seeds[6], 1), 0, 1).astype(jnp.int32),
        "step_index": set_ends(jax.random.randint(seeds[7], (ITERS, S), 0, 4), jax.random.fold_in(seeds[7], 1), 0, 3).astype(jnp.int32),
    }


precise = lax.Precision.HIGHEST

def expand_map(block_rows):
    spread = jnp.repeat(block_rows.astype(jnp.float32), BLK, axis=0)
    return jnp.repeat(spread, BLK, axis=1)

def times_transpose(left, right):
    return lax.dot_general(left, right, (((1,), (1,)), ((), ())), precision=precise, preferred_element_type=jnp.float32)

def times_plain(left, right):
    return jnp.dot(left, right, precision=precise, preferred_element_type=jnp.float32)

def apply_matrix(vector_in, tiles_three, map_three, link_three):
    blocks = vector_in.reshape(S, N_TM, VAR_T).transpose(1, 0, 2)
    bounds = blocks.reshape(N_TM, S, N_COL, COLS_DEV)[..., COLS_DEV - STOR:].reshape(N_TM, S, N_COL * STOR)
    previous = jnp.roll(bounds, 1, axis=0)

    def single(pieces):
        tile_now, map_now, link_now, block_now, prev_now = pieces
        operator = tile_now * expand_map(map_now)
        return times_transpose(block_now, operator) + times_transpose(prev_now, link_now)
    result = lax.map(single, (tiles_three, map_three, link_three, blocks, previous))
    return result.transpose(1, 0, 2).reshape(S, NCON)

def apply_adjoint(dual_in, tiles_three, map_three, link_three):
    blocks = dual_in.reshape(S, N_TM, CON_T).transpose(1, 0, 2)

    def single(pieces):
        tile_now, map_now, link_now, block_now = pieces
        operator = tile_now * expand_map(map_now)
        return (times_plain(block_now, operator), times_plain(block_now, link_now))
    main_part, side_part = lax.map(single, (tiles_three, map_three, link_three, blocks))
    arriving = jnp.roll(side_part, -1, axis=0).reshape(N_TM, S, N_COL, STOR)
    main_four = main_part.reshape(N_TM, S, N_COL, COLS_DEV)
    main_four = jnp.concatenate([main_four[..., :COLS_DEV - STOR], main_four[..., COLS_DEV - STOR:] + arriving], axis=-1)
    return main_four.reshape(N_TM, S, VAR_T).transpose(1, 0, 2).reshape(S, NVAR)

def reference(matrix_tiles, block_map, link_tiles, demand, objective, upper_bound, restart_flag, step_index):
    tiles_three = matrix_tiles.reshape(N_TM, CON_T, VAR_T)
    map_three = block_map.reshape(N_TM, CON_T // BLK, VAR_T // BLK)
    link_three = link_tiles.reshape(N_TM, CON_T, LINKW)
    primal = jnp.zeros((S, NVAR), jnp.float32)
    dual = jnp.zeros((S, NCON), jnp.float32)
    anchor_primal, anchor_dual = (primal, dual)
    avg_primal, avg_dual = (primal, dual)
    count = jnp.zeros((S,), jnp.float32)
    weight_now = jnp.ones((S,), jnp.float32)
    for iteration in range(ITERS):
        eta = 0.15 * (1.0 + step_index[iteration].astype(jnp.float32))
        tau = (eta / weight_now)[:, None]
        sigma = (eta * weight_now)[:, None]
        reduced = objective[None, :] - apply_adjoint(dual, tiles_three, map_three, link_three)
        primal_next = jnp.clip(primal - tau * reduced, 0.0, upper_bound[None, :])
        applied = apply_matrix(2.0 * primal_next - primal, tiles_three, map_three, link_three)
        dual_next = jnp.maximum(dual + sigma * (demand - applied), 0.0)
        count = count + 1.0
        avg_primal = avg_primal + (primal_next - avg_primal) / count[:, None]
        avg_dual = avg_dual + (dual_next - avg_dual) / count[:, None]
        flag = restart_flag[iteration] == 1
        if iteration < ITERS - 1:
            primal_sq = lax.optimization_barrier(jnp.sum(jnp.square(avg_primal - anchor_primal), axis=1))
            dual_sq = lax.optimization_barrier(jnp.sum(jnp.square(avg_dual - anchor_dual), axis=1))
            candidate = jnp.sqrt((dual_sq + 1e-06) / (primal_sq + 1e-06))
            weight_now = jnp.where(flag, jnp.sqrt(weight_now * candidate), weight_now)
        rows_flag = flag[:, None]
        primal = jnp.where(rows_flag, avg_primal, primal_next)
        dual = jnp.where(rows_flag, avg_dual, dual_next)
        anchor_primal = jnp.where(rows_flag, avg_primal, anchor_primal)
        anchor_dual = jnp.where(rows_flag, avg_dual, anchor_dual)
        count = jnp.where(flag, jnp.float32(0.0), count)
    applied = apply_matrix(primal, tiles_three, map_three, link_three)
    violation = jnp.maximum(demand - applied, 0.0)
    reduced = objective[None, :] - apply_adjoint(dual, tiles_three, map_three, link_three)
    viol_sum = lax.optimization_barrier(jnp.sum(jnp.square(violation).reshape(S, N_TM, CON_T), axis=2))
    dual_rows = lax.optimization_barrier(jnp.sum((demand * dual).reshape(S, N_TM, CON_T), axis=2))
    cost_cols = lax.optimization_barrier(jnp.sum((objective[None, :] * primal).reshape(S, N_TM, VAR_T), axis=2))
    bound_cols = lax.optimization_barrier(jnp.sum((upper_bound[None, :] * jnp.minimum(reduced, 0.0)).reshape(S, N_TM, VAR_T), axis=2))
    checks = jnp.stack([jnp.sqrt(viol_sum / CON_T + 1e-06), cost_cols / VAR_T, (dual_rows + bound_cols) / VAR_T], axis=0)
    return (primal, dual, checks.transpose(2, 0, 1))
```

```python
import functools

import jax
import jax.numpy as jnp
from jax import lax
from jax.experimental import pallas as pl
from jax.experimental.pallas import tpu as pltpu
from jax.sharding import PartitionSpec as P

ITERS = 3
CHUNKS = 4
LANES = 128
GROUP = 8
MESH = pl.DeviceIdType.MESH
NN = (((1,), (0,)), ((), ()))
NT = (((1,), (1,)), ((), ()))


def halves(x):
    high = x.astype(jnp.bfloat16)
    return high, (x - high.astype(jnp.float32)).astype(jnp.bfloat16)


def dot(a, b, dims):
    return lax.dot_general(a, b, dims, preferred_element_type=jnp.float32)


def product(left, high, low, dims):
    rows = left.shape[0] // 2
    both = dot(left, high, dims)
    return both[:rows] + (both[rows:] + dot(left[:rows], low, dims))


def stacked(x):
    return jnp.concatenate(halves(x), axis=0)


def column(row, start, size):
    shape = (size, row.shape[1])
    lane = lax.broadcasted_iota(jnp.int32, shape, 1)
    sub = lax.broadcasted_iota(jnp.int32, shape, 0)
    return jnp.sum(jnp.where(lane == sub + start, row, 0.0), axis=1, keepdims=True)


def spread(col, start):
    shape = (col.shape[0], LANES)
    lane = lax.broadcasted_iota(jnp.int32, shape, 1)
    sub = lax.broadcasted_iota(jnp.int32, shape, 0)
    return jnp.sum(jnp.where(lane == sub + start, col, 0.0), axis=0, keepdims=True)


def tile_of(rows):
    sub = lax.broadcasted_iota(jnp.int32, (8, LANES), 0)
    out = jnp.zeros((8, LANES), jnp.float32)
    for i, row in enumerate(rows):
        out = jnp.where(sub == i, row, out)
    return out


def kernel(
    sizes,
    mat, bmap, link, dem, obj, ub, flags, steps,
    primal_out, dual_out, kkt_out,
    kf, lf, kh, kl, lh, ll,
    ybuf, halo, pq, qb, wbuf, pa, side, ab, sb, zbuf,
    xs, xavg, xanc, ds, davg, danc, qx, qavg,
    nsend, ntm, nrow, ncol, fsend, fcol, frow,
    load_sem, out_sem,
    halo0_s, halo0_r, halo_s, halo_r, rsc_s, rsc_r, agc_s, agc_r,
    side_s, side_r, rsr_s, rsr_r, agr_s, agr_r, z_s, z_r,
    ntm_s, ntm_r, nrow_s, nrow_r, ncol_s, ncol_r, fcol_s, fcol_r, frow_s, frow_r,
):
    tms, rws, cls = sizes
    rows, cols = kf.shape
    stor = lf.shape[1]
    edge = cols - stor
    scen = dem.shape[0]
    chunk = cols // CHUNKS
    half = rows // 2
    groups = scen // GROUP
    blk = rows // bmap.shape[0]
    t, r, c = lax.axis_index("tm"), lax.axis_index("row"), lax.axis_index("col")
    g, h = lax.div(c, 2), lax.rem(c, 2)
    own_r = pl.multiple_of(r * GROUP, GROUP)
    own_g = pl.multiple_of(g * GROUP, GROUP)
    own_h = pl.multiple_of(h * half, half)
    order = [CHUNKS - 1] + list(range(CHUNKS - 1))
    pending = []

    def rem(a, n):
        return lax.rem(a, n)

    def at(tm=None, row=None, col=None):
        return {"tm": t if tm is None else tm, "row": r if row is None else row, "col": c if col is None else col}

    def send(src, dst, ssem, rsem, where):
        copy = pltpu.make_async_remote_copy(
            src_ref=src, dst_ref=dst, send_sem=ssem, recv_sem=rsem, device_id=where, device_id_type=MESH
        )
        copy.start()
        pending.append(copy)

    def arrived(dst, ssem, rsem):
        pltpu.make_async_remote_copy(
            src_ref=dst, dst_ref=dst, send_sem=ssem, recv_sem=rsem, device_id=at(), device_id_type=MESH
        ).wait_recv()

    def drain():
        for copy in pending:
            copy.wait_send()
        pending.clear()

    loads = []
    for i in range(rows // blk):
        part = pl.ds(i * blk, blk)
        loads.append(pltpu.make_async_copy(mat.at[part], kf.at[part], load_sem.at[i]))
    loads.append(pltpu.make_async_copy(link, lf, load_sem.at[rows // blk]))
    for copy in loads:
        copy.start()

    before, after = rem(t + tms - 1, tms), rem(t + 1, tms)
    barrier = pltpu.get_barrier_semaphore()
    peers = [at(tm=rem(t + d, tms)) for d in range(1, tms)]
    peers += [at(row=rem(r + d, rws)) for d in range(1, rws)]
    peers += [at(col=rem(c + d, cls)) for d in range(1, cls)]
    peers += [at(tm=x, row=rem(r + d, rws)) for x in (before, after) for d in range(1, rws)]
    for peer in peers:
        pl.semaphore_signal(barrier, inc=1, device_id=peer, device_id_type=MESH)

    weight = jnp.ones((1, scen), jnp.float32)
    count = jnp.zeros((1, scen), jnp.float32)

    def plan(k):
        eta = 0.15 * (1.0 + steps[k : k + 1, :].astype(jnp.float32))
        flag = flags[k : k + 1, :].astype(jnp.float32)
        return eta, flag

    def col_slots():
        for f in (1, 0):
            for dg in range(groups):
                if f == 0 and dg == 0:
                    continue
                hh = h if f == 0 else 1 - h
                yield dg * 2 + f, rem(g + dg, groups), hh, rem(g + groups - dg, groups)

    def send_rows_half(k, f):
        for slot, to_g, hh, _ in col_slots():
            if slot % 2 != f:
                continue
            src = pq.at[k, pl.ds(pl.multiple_of(to_g * GROUP, GROUP), GROUP), pl.ds(pl.multiple_of(hh * half, half), half)]
            send(src, qb.at[k, slot], rsc_s.at[k, slot], rsc_r.at[k, slot], at(col=to_g * 2 + hh))

    def receive_rows(k):
        total = pq[k, pl.ds(own_g, GROUP), pl.ds(own_h, half)]
        for slot, _, _, _ in col_slots():
            arrived(qb.at[k, slot], rsc_s.at[k, slot], rsc_r.at[k, slot])
            total = total + qb[k, slot]
        return total

    def dual_step(k, weight, count, eta, flag):
        sigma = column(eta * weight, own_g, GROUP)
        cnt = column(count, own_g, GROUP)
        flg = column(flag, own_g, GROUP) > 0.5
        q = receive_rows(k)
        mine = dem[pl.ds(own_g, GROUP), pl.ds(own_h, half)]
        if k == 0:
            nxt = jnp.maximum(sigma * (mine - 2.0 * q), 0.0)
            avg, qa = nxt, q
            dual = nxt
            anchor = jnp.zeros_like(nxt)
        else:
            nxt = jnp.maximum(ds[...] + sigma * (mine - (2.0 * q - qx[...])), 0.0)
            avg = davg[...] + (nxt - davg[...]) / cnt
            qa = qavg[...] + (q - qavg[...]) / cnt
            dual = jnp.where(flg, avg, nxt)
            anchor = danc[...]
        ds[...] = dual
        wbuf[k, pl.ds(own_g, GROUP), pl.ds(own_h, half)] = dual
        piece = wbuf.at[k, pl.ds(own_g, GROUP), pl.ds(own_h, half)]
        for slot, to_g, hh, _ in col_slots():
            send(piece, piece, agc_s.at[k, slot], agc_r.at[k, slot], at(col=to_g * 2 + hh))
        davg[...] = avg
        qavg[...] = qa
        q_now = jnp.where(flg, qa, q)
        qx[...] = q_now
        dist = jnp.sum(jnp.square(avg - anchor), axis=1, keepdims=True)
        danc[...] = jnp.where(flg, avg, anchor)
        if k < ITERS - 1:
            return dist
        violation = jnp.sum(jnp.square(jnp.maximum(mine - q_now, 0.0)), axis=1, keepdims=True)
        return violation, jnp.sum(mine * dual, axis=1, keepdims=True)

    def receive_dual(k):
        for slot, _, hh, from_g in col_slots():
            piece = wbuf.at[
                k, pl.ds(pl.multiple_of(from_g * GROUP, GROUP), GROUP), pl.ds(pl.multiple_of(hh * half, half), half)
            ]
            arrived(piece, agc_s.at[k, slot], agc_r.at[k, slot])

    def adjoint_side(k, left):
        side[k] = product(left, lh[...], ll[...], NN)
        for d in range(rws):
            to_r = rem(r + d, rws)
            src = side.at[k, pl.ds(pl.multiple_of(to_r * GROUP, GROUP), GROUP)]
            send(src, sb.at[k, d], side_s.at[k, d], side_r.at[k, d], at(tm=before, row=to_r))

    def adjoint_chunk(k, j, left):
        part = pl.ds(j * chunk, chunk)
        pa[k, :, part] = product(left, kh[:, part], kl[:, part], NN)
        for d in (2, 1, 3):
            to_r = rem(r + d, rws)
            src = pa.at[k, pl.ds(pl.multiple_of(to_r * GROUP, GROUP), GROUP), part]
            send(src, ab.at[k, d, :, part], rsr_s.at[k, j, d], rsr_r.at[k, j, d], at(row=to_r))

    def receive_adjoint(k, j):
        part = pl.ds(j * chunk, chunk)
        total = pa[k, pl.ds(own_r, GROUP), part]
        for d in (1, 3, 2):
            arrived(ab.at[k, d, :, part], rsr_s.at[k, j, d], rsr_r.at[k, j, d])
            total = total + ab[k, d, :, part]
        if j == CHUNKS - 1:
            extra = None
            for d in range(rws):
                arrived(sb.at[k, d], side_s.at[k, d], side_r.at[k, d])
                extra = sb[k, d] if extra is None else extra + sb[k, d]
            total = jnp.concatenate([total[:, : chunk - stor], total[:, chunk - stor :] + extra], axis=1)
        return total

    def primal_steps(k, weight, eta):
        tau = column(eta / weight, own_r, GROUP)
        for j in order:
            part = pl.ds(j * chunk, chunk)
            reduced = obj[:, part] - receive_adjoint(k - 1, j)
            ybuf[k, pl.ds(own_r, GROUP), part] = jnp.clip(xs[:, part] - tau * reduced, 0.0, ub[:, part])
            piece = ybuf.at[k, pl.ds(own_r, GROUP), part]
            for d in (2, 1, 3):
                send(piece, piece, agr_s.at[k, j, d], agr_r.at[k, j, d], at(row=rem(r + d, rws)))
            if j == CHUNKS - 1:
                for d in range(rws):
                    send(
                        ybuf.at[k, pl.ds(own_r, GROUP), pl.ds(edge, stor)],
                        halo.at[k, pl.ds(own_r, GROUP)],
                        halo_s.at[k, d], halo_r.at[k, d], at(tm=after, row=rem(r + d, rws)),
                    )

    def primal_rest(k, count, flag):
        cnt = column(count, own_r, GROUP)
        flg = column(flag, own_r, GROUP) > 0.5
        nxt = ybuf[k, pl.ds(own_r, GROUP), :]
        if k == 0:
            avg = nxt
            anchor = jnp.zeros_like(nxt)
        else:
            avg = xavg[...] + (nxt - xavg[...]) / cnt
            anchor = xanc[...]
        now = jnp.where(flg, avg, nxt)
        xs[...] = now
        xavg[...] = avg
        dist = jnp.sum(jnp.square(avg - anchor), axis=1, keepdims=True)
        xanc[...] = jnp.where(flg, avg, anchor)
        if k < ITERS - 1:
            return dist
        zbuf[pl.ds(own_r, GROUP), :] = now
        piece = zbuf.at[pl.ds(own_r, GROUP)]
        for d in (2, 1, 3):
            send(piece, piece, z_s.at[d], z_r.at[d], at(row=rem(r + d, rws)))
        return jnp.sum(obj[...] * now, axis=1, keepdims=True)

    def receive_primal(k, j):
        part = pl.ds(j * chunk, chunk)
        for d in (1, 3, 2):
            piece = ybuf.at[k, pl.ds(pl.multiple_of(rem(r + rws - d, rws) * GROUP, GROUP), GROUP), part]
            arrived(piece, agr_s.at[k, j, d], agr_r.at[k, j, d])

    def apply_chunks(k):
        acc = None
        for j in order:
            receive_primal(k, j)
            part = pl.ds(j * chunk, chunk)
            left = stacked(ybuf[k, :, part])
            if j != order[-1]:
                term = product(left, kh[:, part], kl[:, part], NT)
                if j == CHUNKS - 1:
                    for d in range(rws):
                        from_r = pl.multiple_of(rem(r + rws - d, rws) * GROUP, GROUP)
                        arrived(halo.at[k, pl.ds(from_r, GROUP)], halo_s.at[k, d], halo_r.at[k, d])
                    pq[k] = term + product(stacked(halo[k]), lh[...], ll[...], NT)
                else:
                    pq[k] = pq[k] + term
            else:
                for f in (1, 0):
                    hh = pl.multiple_of((h if f == 0 else 1 - h) * half, half)
                    some = pl.ds(hh, half)
                    pq[k, :, some] = pq[k, :, some] + product(left, kh[some, part], kl[some, part], NT)
                    send_rows_half(k, f)

    def norm_tm(k, dx, dy):
        nsend[k, 0] = tile_of([spread(dx, own_r), spread(dy, own_g)])
        for d in range(1, tms):
            send(nsend.at[k, 0], ntm.at[k, d], ntm_s.at[k, d], ntm_r.at[k, d], at(tm=rem(t + d, tms)))

    def norm_row(k):
        total = nsend[k, 0]
        for d in range(1, tms):
            arrived(ntm.at[k, d], ntm_s.at[k, d], ntm_r.at[k, d])
            total = total + ntm[k, d]
        nsend[k, 1] = total
        for d in range(1, rws):
            send(nsend.at[k, 1], nrow.at[k, d], nrow_s.at[k, d], nrow_r.at[k, d], at(row=rem(r + d, rws)))

    def norm_col(k):
        total = nsend[k, 1]
        for d in range(1, rws):
            arrived(nrow.at[k, d], nrow_s.at[k, d], nrow_r.at[k, d])
            total = total + nrow[k, d]
        nsend[k, 2] = total
        for d in range(1, cls):
            send(nsend.at[k, 2], ncol.at[k, d], ncol_s.at[k, d], ncol_r.at[k, d], at(col=rem(c + d, cls)))

    def norm_weight(k, weight, flag):
        total = nsend[k, 2]
        for d in range(1, cls):
            arrived(ncol.at[k, d], ncol_s.at[k, d], ncol_r.at[k, d])
            total = total + ncol[k, d]
        dx, dy = total[0:1, 0:scen], total[1:2, 0:scen]
        candidate = jnp.sqrt((dy + 1e-06) / (dx + 1e-06))
        return jnp.where(flag > 0.5, jnp.sqrt(weight * candidate), weight)

    eta, flag = plan(0)
    count = count + 1.0
    tau_all = column(eta, 0, scen)
    ybuf[0] = jnp.clip(-tau_all * obj[...], 0.0, ub[...])
    left0 = stacked(ybuf[0])
    for i in range(rows // blk):
        loads[i].wait()
        part = pl.ds(i * blk, blk)
        for j in range(cols // blk):
            across = pl.ds(j * blk, blk)
            high, low = halves(kf[part, across] * bmap[i, j].astype(jnp.float32))
            kh[part, across] = high
            kl[part, across] = low
        if i == 0:
            pl.semaphore_wait(barrier, len(peers))
            send(ybuf.at[0, :, pl.ds(edge, stor)], halo.at[0], halo0_s, halo0_r, at(tm=after))
        pq[0, :, part] = product(left0, kh[part, :], kl[part, :], NT)
    loads[-1].wait()
    high, low = halves(lf[...])
    lh[...] = high
    ll[...] = low
    arrived(halo.at[0], halo0_s, halo0_r)
    left0 = stacked(halo[0])
    for f in (1, 0):
        some = pl.ds(pl.multiple_of((h if f == 0 else 1 - h) * half, half), half)
        pq[0, :, some] = pq[0, :, some] + product(left0, lh[some, :], ll[some, :], NT)
        send_rows_half(0, f)
    dx = primal_rest(0, count, flag)

    for k in range(ITERS):
        if k > 0:
            eta, flag = plan(k)
            count = count + 1.0
            primal_steps(k, weight, eta)
            dx = primal_rest(k, count, flag)
            apply_chunks(k)
        if k < ITERS - 1:
            dy = dual_step(k, weight, count, eta, flag)
            norm_tm(k, dx, dy)
        else:
            viol, dual_part = dual_step(k, weight, count, eta, flag)
        drain_now, pending[:] = pending[:], []
        receive_dual(k)
        left = stacked(wbuf[k])
        adjoint_side(k, left)
        for n, j in enumerate(order):
            adjoint_chunk(k, j, left)
            if k < ITERS - 1 and n == 1:
                norm_row(k)
        for copy in drain_now:
            copy.wait_send()
        if k < ITERS - 1:
            norm_col(k)
            weight = norm_weight(k, weight, flag)
            count = jnp.where(flag > 0.5, 0.0, count)

    k = ITERS - 1
    dual_copy = pltpu.make_async_copy(wbuf.at[k], dual_out, out_sem.at[0])
    dual_copy.start()
    for d in (1, 3, 2):
        from_r = pl.multiple_of(rem(r + rws - d, rws) * GROUP, GROUP)
        arrived(zbuf.at[pl.ds(from_r, GROUP)], z_s.at[d], z_r.at[d])
    primal_copy = pltpu.make_async_copy(zbuf, primal_out, out_sem.at[1])
    primal_copy.start()
    bound = jnp.zeros((GROUP, 1), jnp.float32)
    for j in order:
        part = pl.ds(j * chunk, chunk)
        reduced = obj[:, part] - receive_adjoint(k, j)
        bound = bound + jnp.sum(ub[:, part] * jnp.minimum(reduced, 0.0), axis=1, keepdims=True)
    cost = dx
    fcol[c] = tile_of([spread(viol, own_g), spread(dual_part, own_g), spread(cost, own_r), spread(bound, own_r)])
    for d in range(1, cls):
        send(fcol.at[c], fcol.at[c], fcol_s.at[d], fcol_r.at[d], at(col=rem(c + d, cls)))
    drain_now, pending[:] = pending[:], []
    for d in range(1, cls):
        arrived(fcol.at[rem(c + cls - d, cls)], fcol_s.at[d], fcol_r.at[d])
    total = fcol[0]
    for i in range(1, cls):
        total = total + fcol[i]
    frow[r] = total
    for d in range(1, rws):
        send(frow.at[r], frow.at[r], frow_s.at[d], frow_r.at[d], at(row=rem(r + d, rws)))
    for copy in drain_now:
        copy.wait_send()
    for d in range(1, rws):
        arrived(frow.at[rem(r + rws - d, rws)], frow_s.at[d], frow_r.at[d])
    total = frow[0]
    for i in range(1, rws):
        total = total + frow[i]
    con_total, var_total = float(rows * rws), float(cols * cls)
    kkt_out[0, 0:1, :] = jnp.sqrt(total[0:1, 0:scen] / con_total + 1e-06)
    kkt_out[0, 1:2, :] = total[2:3, 0:scen] / var_total
    kkt_out[0, 2:3, :] = (total[1:2, 0:scen] + total[3:4, 0:scen]) / var_total
    drain()
    dual_copy.wait()
    primal_copy.wait()


def on_device(matrix_tiles, block_map, link_tiles, demand, objective, upper_bound, restart_flag, step_index):
    rows, cols = matrix_tiles.shape
    stor = link_tiles.shape[1]
    scen = demand.shape[0]
    tms, rws, cls = lax.axis_size("tm"), lax.axis_size("row"), lax.axis_size("col")
    half = rows // 2
    f32, bf16 = jnp.float32, jnp.bfloat16
    vmem = pl.BlockSpec(memory_space=pltpu.VMEM)
    smem = pl.BlockSpec(memory_space=pltpu.SMEM)
    anywhere = pl.BlockSpec(memory_space=pl.ANY)
    V = pltpu.VMEM
    D = pltpu.SemaphoreType.DMA
    n = ITERS
    scratch = [
        V((rows, cols), f32), V((rows, stor), f32),
        V((rows, cols), bf16), V((rows, cols), bf16), V((rows, stor), bf16), V((rows, stor), bf16),
        V((n, scen, cols), f32), V((n, scen, stor), f32), V((n, scen, rows), f32), V((n, cls, GROUP, half), f32),
        V((n, scen, rows), f32), V((n, scen, cols), f32), V((n, scen, stor), f32),
        V((n, rws, GROUP, cols), f32), V((n, rws, GROUP, stor), f32), V((scen, cols), f32),
        V((GROUP, cols), f32), V((GROUP, cols), f32), V((GROUP, cols), f32),
        V((GROUP, half), f32), V((GROUP, half), f32), V((GROUP, half), f32), V((GROUP, half), f32), V((GROUP, half), f32),
        V((n - 1, 3, 8, LANES), f32), V((n - 1, tms, 8, LANES), f32), V((n - 1, rws, 8, LANES), f32),
        V((n - 1, cls, 8, LANES), f32), V((8, LANES), f32), V((cls, 8, LANES), f32), V((rws, 8, LANES), f32),
        D((rows // (rows // block_map.shape[0]) + 1,)), D((2,)),
        D(()), D(()), D((n, rws)), D((n, rws)), D((n, cls)), D((n, cls)), D((n, cls)), D((n, cls)),
        D((n, rws)), D((n, rws)), D((n, CHUNKS, rws)), D((n, CHUNKS, rws)),
        D((n, CHUNKS, rws)), D((n, CHUNKS, rws)), D((rws,)), D((rws,)),
        D((n - 1, tms)), D((n - 1, tms)), D((n - 1, rws)), D((n - 1, rws)), D((n - 1, cls)), D((n - 1, cls)),
        D((cls,)), D((cls,)), D((rws,)), D((rws,)),
    ]
    return pl.pallas_call(
        functools.partial(kernel, (tms, rws, cls)),
        out_shape=(
            jax.ShapeDtypeStruct((scen, cols), f32),
            jax.ShapeDtypeStruct((scen, rows), f32),
            jax.ShapeDtypeStruct((1, 3, scen), f32),
        ),
        in_specs=[anywhere, smem, anywhere, vmem, vmem, vmem, vmem, vmem],
        out_specs=(anywhere, anywhere, vmem),
        scratch_shapes=scratch,
        compiler_params=pltpu.CompilerParams(
            collective_id=0, has_side_effects=True, vmem_limit_bytes=48 << 20
        ),
        name="pdhg",
    )(
        matrix_tiles, block_map, link_tiles, demand, objective.reshape(1, cols), upper_bound.reshape(1, cols),
        restart_flag, step_index,
    )


def solution(mesh):
    in_specs = (
        P(("tm", "row"), "col"),
        P(("tm", "row"), "col"),
        P(("tm", "row"), "col"),
        P(None, ("tm", "row")),
        P(("tm", "col")),
        P(("tm", "col")),
        P(),
        P(),
    )
    out_specs = (P(None, ("tm", "col")), P(None, ("tm", "row")), P("tm", None, None))
    return jax.shard_map(
        on_device, mesh=mesh, in_specs=in_specs, out_specs=out_specs, check_vma=False
    )
```

```python
import functools

import jax
import jax.numpy as jnp
from jax import lax
from jax.experimental import pallas as pl
from jax.experimental.pallas import tpu as pltpu
from jax.sharding import PartitionSpec as P

ITERS = 3
CHUNKS = 4
LANES = 128
GROUP = 8
MESH = pl.DeviceIdType.MESH
NN = (((1,), (0,)), ((), ()))
NT = (((1,), (1,)), ((), ()))


def halves(x):
    high = x.astype(jnp.bfloat16)
    return high, (x - high.astype(jnp.float32)).astype(jnp.bfloat16)


def dot(a, b, dims):
    return lax.dot_general(a, b, dims, preferred_element_type=jnp.float32)


def product(left, high, low, dims):
    rows = left.shape[0] // 2
    both = dot(left, high, dims)
    return both[:rows] + (both[rows:] + dot(left[:rows], low, dims))


def stacked(x):
    return jnp.concatenate(halves(x), axis=0)


def column(row, start, size):
    shape = (size, row.shape[1])
    lane = lax.broadcasted_iota(jnp.int32, shape, 1)
    sub = lax.broadcasted_iota(jnp.int32, shape, 0)
    return jnp.sum(jnp.where(lane == sub + start, row, 0.0), axis=1, keepdims=True)


def spread(col, start):
    shape = (col.shape[0], LANES)
    lane = lax.broadcasted_iota(jnp.int32, shape, 1)
    sub = lax.broadcasted_iota(jnp.int32, shape, 0)
    return jnp.sum(jnp.where(lane == sub + start, col, 0.0), axis=0, keepdims=True)


def kernel(
    sizes,
    mat, bmap_in, link, dem_in, obj_in, ub_in, flags_in, steps_in,
    primal_out, dual_out, kkt_out,
    bmap, flags, steps, dem, costs, far,
    kf, lf, kh, kl, lh, ll,
    ybuf, ypiece, halo, pq, qb, wbuf, pa, side, ab, sb, zbuf, zpiece,
    xs, xavg, xanc, ds, davg, danc, qx, qavg,
    nsend, near_buf, wide_buf, fpart, fcol, fsum, frow,
    load_sem, small_sem, out_sem, pair_sem,
    halo_s, halo_r, rsc_s, rsc_r, agc_s, agc_r,
    side_s, side_r, rsr_s, rsr_r, agr_s, agr_r, z_s, z_r,
    near_s, near_r, wide_s, wide_r, fcol_s, fcol_r, frow_s, frow_r,
):
    tms, rws, cls = sizes
    rows, cols = kf.shape
    stor = lf.shape[1]
    edge = cols - stor
    scen = ybuf.shape[1]
    chunk = cols // CHUNKS
    half = rows // 2
    groups = scen // GROUP
    blk = rows // bmap.shape[0]
    t, r, c = lax.axis_index("tm"), lax.axis_index("row"), lax.axis_index("col")
    g, h = lax.div(c, 2), lax.rem(c, 2)
    o = lax.rem(t + tms // 2, tms)
    own_r = pl.multiple_of(r * GROUP, GROUP)
    own_g = pl.multiple_of(g * GROUP, GROUP)
    own_h = pl.multiple_of(h * half, half)
    near_first = (0, 1, 3, 2)
    far_first = near_first[::-1]
    order = [CHUNKS - 1] + list(range(CHUNKS - 1))
    pending = []

    def rem(a, n):
        return lax.rem(a, n)

    def at(tm=None, row=None, col=None):
        return {"tm": t if tm is None else tm, "row": r if row is None else row, "col": c if col is None else col}

    def send(src, dst, ssem, rsem, where):
        copy = pltpu.make_async_remote_copy(
            src_ref=src, dst_ref=dst, send_sem=ssem, recv_sem=rsem, device_id=where, device_id_type=MESH
        )
        copy.start()
        pending.append(copy)

    def arrived(dst, ssem, rsem):
        pltpu.make_async_remote_copy(
            src_ref=dst, dst_ref=dst, send_sem=ssem, recv_sem=rsem, device_id=at(), device_id_type=MESH
        ).wait_recv()

    def drain():
        for copy in pending:
            copy.wait_send()
        pending.clear()

    small = [
        pltpu.make_async_copy(src, dst, small_sem.at[i])
        for i, (src, dst) in enumerate(
            (
                (steps_in, steps), (obj_in, costs.at[0]), (ub_in, costs.at[1]), (bmap_in, bmap), (flags_in, flags),
                (dem_in.at[pl.ds(own_g, GROUP), pl.ds(own_h, half)], dem),
            )
        )
    ]
    loads = []
    for i in range(rows // blk):
        part = pl.ds(i * blk, blk)
        loads.append(pltpu.make_async_copy(mat.at[part], kf.at[part], load_sem.at[i]))
    loads.append(pltpu.make_async_copy(link, lf, load_sem.at[rows // blk]))
    for copy in small + loads:
        copy.start()

    def near_peers():
        for dt in range(tms):
            for f in range(2):
                if dt or f:
                    yield dt * 2 + f, at(tm=rem(t + dt, tms), col=g * 2 + (1 - h if f else h))

    def wide_peers():
        for dr in (2, 1, 3, 0):
            for dg in range(groups):
                if dr or dg:
                    yield dr * groups + dg, at(row=rem(r + dr, rws), col=rem(g + dg, groups) * 2 + h)

    behind, ahead = rem(o + tms - 1, tms), rem(o + 1, tms)
    barrier = pltpu.get_barrier_semaphore()
    peers = [at(tm=x, row=rem(r + d, rws)) for d in (2, 1, 3) for x in (o, behind, ahead)]
    peers += [place for _, place in wide_peers()]
    peers += [place for _, place in near_peers()]
    peers += [at(col=rem(g + dg, groups) * 2 + 1 - h) for dg in range(1, groups)]
    for peer in peers:
        pl.semaphore_signal(barrier, inc=1, device_id=peer, device_id_type=MESH)

    weight = jnp.ones((1, scen), jnp.float32)
    count = jnp.zeros((1, scen), jnp.float32)

    def plan(k):
        eta = 0.15 * (1.0 + steps[k : k + 1, :].astype(jnp.float32))
        flag = flags[k : k + 1, :].astype(jnp.float32)
        return eta, flag

    def col_slots():
        for f in (1, 0):
            for dg in range(groups):
                if f == 0 and dg == 0:
                    continue
                hh = h if f == 0 else 1 - h
                yield dg * 2 + f, rem(g + dg, groups), hh, rem(g + groups - dg, groups)

    def send_rows_half(k, f):
        for slot, to_g, hh, _ in col_slots():
            if slot % 2 != f:
                continue
            src = pq.at[k, pl.ds(pl.multiple_of(to_g * GROUP, GROUP), GROUP), pl.ds(pl.multiple_of(hh * half, half), half)]
            send(src, qb.at[k, slot], rsc_s.at[k, slot], rsc_r.at[k, slot], at(col=to_g * 2 + hh))

    def receive_rows(k):
        total = pq[k, pl.ds(own_g, GROUP), pl.ds(own_h, half)]
        for slot, _, _, _ in col_slots():
            arrived(qb.at[k, slot], rsc_s.at[k, slot], rsc_r.at[k, slot])
            total = total + qb[k, slot]
        return total

    def dual_step(k, weight, count, eta, flag):
        sigma = column(eta * weight, own_g, GROUP)
        cnt = column(count, own_g, GROUP)
        flg = column(flag, own_g, GROUP) > 0.5
        q = receive_rows(k)
        mine = dem[...]
        if k == 0:
            nxt = jnp.maximum(sigma * (mine - 2.0 * q), 0.0)
            avg, qa = nxt, q
            dual = nxt
            anchor = jnp.zeros_like(nxt)
        else:
            nxt = jnp.maximum(ds[...] + sigma * (mine - (2.0 * q - qx[...])), 0.0)
            avg = davg[...] + (nxt - davg[...]) / cnt
            qa = qavg[...] + (q - qavg[...]) / cnt
            dual = jnp.where(flg, avg, nxt)
            anchor = danc[...]
        ds[...] = dual
        wbuf[k, pl.ds(own_g, GROUP), pl.ds(own_h, half)] = dual
        piece = wbuf.at[k, pl.ds(own_g, GROUP), pl.ds(own_h, half)]
        for slot, to_g, hh, _ in col_slots():
            send(piece, piece, agc_s.at[k, slot], agc_r.at[k, slot], at(col=to_g * 2 + hh))
        davg[...] = avg
        qavg[...] = qa
        q_now = jnp.where(flg, qa, q)
        qx[...] = q_now
        dist = jnp.sum(jnp.square(avg - anchor), axis=1, keepdims=True)
        danc[...] = jnp.where(flg, avg, anchor)
        if k < ITERS - 1:
            return dist
        violation = jnp.sum(jnp.square(jnp.maximum(mine - q_now, 0.0)), axis=1, keepdims=True)
        return violation, jnp.sum(mine * dual, axis=1, keepdims=True)

    def receive_dual(k):
        for slot, _, hh, from_g in col_slots():
            piece = wbuf.at[
                k, pl.ds(pl.multiple_of(from_g * GROUP, GROUP), GROUP), pl.ds(pl.multiple_of(hh * half, half), half)
            ]
            arrived(piece, agc_s.at[k, slot], agc_r.at[k, slot])

    def adjoint_side(k, left):
        side[k] = product(left, lh[...], ll[...], NN)
        for d in range(rws):
            to_r = rem(r + d, rws)
            src = side.at[k, pl.ds(pl.multiple_of(to_r * GROUP, GROUP), GROUP)]
            send(src, sb.at[k, d], side_s.at[k, d], side_r.at[k, d], at(tm=behind, row=to_r))

    def adjoint_chunk(k, j, left):
        part = pl.ds(j * chunk, chunk)
        pa[k, :, part] = product(left, kh[:, part], kl[:, part], NN)
        for d in far_first:
            to_r = rem(r + d, rws)
            src = pa.at[k, pl.ds(pl.multiple_of(to_r * GROUP, GROUP), GROUP), part]
            send(src, ab.at[k, d, :, part], rsr_s.at[k, j, d], rsr_r.at[k, j, d], at(tm=o, row=to_r))

    def receive_adjoint(k, j):
        part = pl.ds(j * chunk, chunk)
        total = None
        for d in near_first:
            arrived(ab.at[k, d, :, part], rsr_s.at[k, j, d], rsr_r.at[k, j, d])
            total = ab[k, d, :, part] if total is None else total + ab[k, d, :, part]
        if j == CHUNKS - 1:
            extra = None
            for d in range(rws):
                arrived(sb.at[k, d], side_s.at[k, d], side_r.at[k, d])
                extra = sb[k, d] if extra is None else extra + sb[k, d]
            total = jnp.concatenate([total[:, : chunk - stor], total[:, chunk - stor :] + extra], axis=1)
        return total

    def primal_steps(k, weight, eta):
        tau = column(eta / weight, own_r, GROUP)
        for j in order:
            part = pl.ds(j * chunk, chunk)
            reduced = far[0, :, part] - receive_adjoint(k - 1, j)
            ypiece[k, :, part] = jnp.clip(xs[:, part] - tau * reduced, 0.0, far[1, :, part])
            for d in far_first:
                send(
                    ypiece.at[k, :, part], ybuf.at[k, pl.ds(own_r, GROUP), part],
                    agr_s.at[k, j, d], agr_r.at[k, j, d], at(tm=o, row=rem(r + d, rws)),
                )
            if j == CHUNKS - 1:
                for d in far_first:
                    send(
                        ypiece.at[k, :, pl.ds(edge, stor)], halo.at[k, pl.ds(own_r, GROUP)],
                        halo_s.at[k, d], halo_r.at[k, d], at(tm=ahead, row=rem(r + d, rws)),
                    )

    def primal_rest(k, count, flag):
        cnt = column(count, own_r, GROUP)
        flg = column(flag, own_r, GROUP) > 0.5
        nxt = ypiece[k]
        if k == 0:
            avg = nxt
            anchor = jnp.zeros_like(nxt)
        else:
            avg = xavg[...] + (nxt - xavg[...]) / cnt
            anchor = xanc[...]
        now = jnp.where(flg, avg, nxt)
        xs[...] = now
        xavg[...] = avg
        dist = jnp.sum(jnp.square(avg - anchor), axis=1, keepdims=True)
        xanc[...] = jnp.where(flg, avg, anchor)
        if k < ITERS - 1:
            return dist
        zpiece[...] = now
        for d in far_first:
            send(zpiece, zbuf.at[pl.ds(own_r, GROUP)], z_s.at[d], z_r.at[d], at(tm=o, row=rem(r + d, rws)))
        return jnp.sum(far[0] * now, axis=1, keepdims=True)

    def receive_primal(k, j):
        part = pl.ds(j * chunk, chunk)
        for d in near_first:
            piece = ybuf.at[k, pl.ds(pl.multiple_of(rem(r + rws - d, rws) * GROUP, GROUP), GROUP), part]
            arrived(piece, agr_s.at[k, j, d], agr_r.at[k, j, d])

    def apply_chunks(k):
        acc = None
        for j in order:
            receive_primal(k, j)
            part = pl.ds(j * chunk, chunk)
            left = stacked(ybuf[k, :, part])
            if j != order[-1]:
                term = product(left, kh[:, part], kl[:, part], NT)
                if j == CHUNKS - 1:
                    for d in range(rws):
                        from_r = pl.multiple_of(rem(r + rws - d, rws) * GROUP, GROUP)
                        arrived(halo.at[k, pl.ds(from_r, GROUP)], halo_s.at[k, d], halo_r.at[k, d])
                    pq[k] = term + product(stacked(halo[k]), lh[...], ll[...], NT)
                else:
                    pq[k] = pq[k] + term
            else:
                for f in (1, 0):
                    hh = pl.multiple_of((h if f == 0 else 1 - h) * half, half)
                    some = pl.ds(hh, half)
                    pq[k, :, some] = pq[k, :, some] + product(left, kh[some, part], kl[some, part], NT)
                    send_rows_half(k, f)

    def norm_start(k, dx, dy):
        nsend[k, 0] = spread(dx, own_r) + spread(dy, scen + own_g)
        for slot, place in near_peers():
            send(nsend.at[k, 0], near_buf.at[k, slot], near_s.at[k, slot], near_r.at[k, slot], place)

    def norm_middle(k):
        total = nsend[k, 0]
        for slot, _ in near_peers():
            arrived(near_buf.at[k, slot], near_s.at[k, slot], near_r.at[k, slot])
            total = total + near_buf[k, slot]
        nsend[k, 1] = total
        for slot, place in wide_peers():
            send(nsend.at[k, 1], wide_buf.at[k, slot], wide_s.at[k, slot], wide_r.at[k, slot], place)

    def norm_weight(k, weight, flag):
        total = nsend[k, 1]
        for slot, _ in wide_peers():
            arrived(wide_buf.at[k, slot], wide_s.at[k, slot], wide_r.at[k, slot])
            total = total + wide_buf[k, slot]
        dx, dy = total[:, 0:scen], total[:, scen : 2 * scen]
        candidate = jnp.sqrt((dy + 1e-06) / (dx + 1e-06))
        return jnp.where(flag > 0.5, jnp.sqrt(weight * candidate), weight)

    for copy in small:
        copy.wait()
    eta, flag = plan(0)
    count = count + 1.0
    ybuf[0] = jnp.clip(-column(eta, 0, scen) * costs[0], 0.0, costs[1])
    left0 = stacked(ybuf[0])
    for i in range(rows // blk):
        loads[i].wait()
        part = pl.ds(i * blk, blk)
        for j in range(cols // blk):
            across = pl.ds(j * blk, blk)
            high, low = halves(kf[part, across] * bmap[i, j].astype(jnp.float32))
            kh[part, across] = high
            kl[part, across] = low
        pq[0, :, part] = product(left0, kh[part, :], kl[part, :], NT)
        if i == 1:
            pl.semaphore_wait(barrier, len(peers))
            send(ybuf.at[0, :, pl.ds(edge, stor)], halo.at[0], pair_sem.at[0], pair_sem.at[1], at(tm=rem(t + 1, tms)))
            send(costs, far, pair_sem.at[2], pair_sem.at[3], at(tm=o))
    loads[-1].wait()
    high, low = halves(lf[...])
    lh[...] = high
    ll[...] = low
    arrived(halo.at[0], pair_sem.at[0], pair_sem.at[1])
    left0 = stacked(halo[0])
    for f in (1, 0):
        some = pl.ds(pl.multiple_of((h if f == 0 else 1 - h) * half, half), half)
        pq[0, :, some] = pq[0, :, some] + product(left0, lh[some, :], ll[some, :], NT)
        send_rows_half(0, f)
    arrived(far, pair_sem.at[2], pair_sem.at[3])
    ypiece[0] = jnp.clip(-column(eta, own_r, GROUP) * far[0], 0.0, far[1])
    dx = primal_rest(0, count, flag)

    for k in range(ITERS):
        if k > 0:
            eta, flag = plan(k)
            count = count + 1.0
            primal_steps(k, weight, eta)
            dx = primal_rest(k, count, flag)
            apply_chunks(k)
        if k < ITERS - 1:
            dy = dual_step(k, weight, count, eta, flag)
            norm_start(k, dx, dy)
        else:
            viol, dual_part = dual_step(k, weight, count, eta, flag)
            fpart[0] = spread(viol, own_g) + spread(dual_part, scen + own_g)
            send(fpart.at[0], fpart.at[1], pair_sem.at[4], pair_sem.at[5], at(tm=o))
        drain_now, pending[:] = pending[:], []
        receive_dual(k)
        left = stacked(wbuf[k])
        adjoint_side(k, left)
        for n, j in enumerate(order):
            adjoint_chunk(k, j, left)
            if k < ITERS - 1 and n == 0:
                norm_middle(k)
        for copy in drain_now:
            copy.wait_send()
        if k < ITERS - 1:
            weight = norm_weight(k, weight, flag)
            count = jnp.where(flag > 0.5, 0.0, count)

    k = ITERS - 1
    dual_copy = pltpu.make_async_copy(wbuf.at[k], dual_out, out_sem.at[0])
    dual_copy.start()
    for d in near_first:
        from_r = pl.multiple_of(rem(r + rws - d, rws) * GROUP, GROUP)
        arrived(zbuf.at[pl.ds(from_r, GROUP)], z_s.at[d], z_r.at[d])
    primal_copy = pltpu.make_async_copy(zbuf, primal_out, out_sem.at[1])
    primal_copy.start()
    arrived(fpart.at[1], pair_sem.at[4], pair_sem.at[5])
    fixed = fpart[1] + spread(dx, 2 * scen + own_r)
    bound = jnp.zeros((GROUP, 1), jnp.float32)
    for j in order:
        part = pl.ds(j * chunk, chunk)
        reduced = far[0, :, part] - receive_adjoint(k, j)
        bound = bound + jnp.sum(far[1, :, part] * jnp.minimum(reduced, 0.0), axis=1, keepdims=True)
    fcol[c] = fixed + spread(bound, 3 * scen + own_r)
    for d in range(1, cls):
        send(fcol.at[c], fcol.at[c], fcol_s.at[d], fcol_r.at[d], at(col=rem(c + d, cls)))
    drain_now, pending[:] = pending[:], []
    for copy in drain_now[:-7]:
        copy.wait_send()
    for d in range(1, cls):
        arrived(fcol.at[rem(c + cls - d, cls)], fcol_s.at[d], fcol_r.at[d])
    total = fcol[0]
    for i in range(1, cls):
        total = total + fcol[i]
    fsum[...] = total
    for d in far_first:
        send(fsum, frow.at[r], frow_s.at[d], frow_r.at[d], at(tm=o, row=rem(r + d, rws)))
    for copy in drain_now[-7:]:
        copy.wait_send()
    dual_copy.wait()
    primal_copy.wait()
    for d in near_first:
        arrived(frow.at[rem(r + rws - d, rws)], frow_s.at[d], frow_r.at[d])
    total = frow[0]
    for i in range(1, rws):
        total = total + frow[i]
    con_total, var_total = float(rows * rws), float(cols * cls)
    parts = [total[:, i * scen : (i + 1) * scen] for i in range(4)]
    kkt_out[0, 0:1, :] = jnp.sqrt(parts[0] / con_total + 1e-06)
    kkt_out[0, 1:2, :] = parts[2] / var_total
    kkt_out[0, 2:3, :] = (parts[1] + parts[3]) / var_total
    drain()


def on_device(matrix_tiles, block_map, link_tiles, demand, objective, upper_bound, restart_flag, step_index):
    rows, cols = matrix_tiles.shape
    stor = link_tiles.shape[1]
    scen = demand.shape[0]
    tms, rws, cls = lax.axis_size("tm"), lax.axis_size("row"), lax.axis_size("col")
    half = rows // 2
    groups = scen // GROUP
    f32, bf16 = jnp.float32, jnp.bfloat16
    vmem = pl.BlockSpec(memory_space=pltpu.VMEM)
    hbm = pl.BlockSpec(memory_space=pltpu.HBM)
    V = pltpu.VMEM
    D = pltpu.SemaphoreType.DMA
    n = ITERS
    scratch = [
        pltpu.SMEM(block_map.shape, jnp.int32), V(restart_flag.shape, jnp.int32), V(step_index.shape, jnp.int32),
        V((GROUP, half), f32), V((2, 1, cols), f32), V((2, 1, cols), f32),
        V((rows, cols), f32), V((rows, stor), f32),
        V((rows, cols), bf16), V((rows, cols), bf16), V((rows, stor), bf16), V((rows, stor), bf16),
        V((n, scen, cols), f32), V((n, GROUP, cols), f32), V((n, scen, stor), f32), V((n, scen, rows), f32),
        V((n, cls, GROUP, half), f32),
        V((n, scen, rows), f32), V((n, scen, cols), f32), V((n, scen, stor), f32),
        V((n, rws, GROUP, cols), f32), V((n, rws, GROUP, stor), f32), V((scen, cols), f32), V((GROUP, cols), f32),
        V((GROUP, cols), f32), V((GROUP, cols), f32), V((GROUP, cols), f32),
        V((GROUP, half), f32), V((GROUP, half), f32), V((GROUP, half), f32), V((GROUP, half), f32), V((GROUP, half), f32),
        V((n - 1, 2, 1, LANES), f32), V((n - 1, 2 * tms, 1, LANES), f32), V((n - 1, groups * rws, 1, LANES), f32),
        V((2, 1, LANES), f32), V((cls, 1, LANES), f32), V((1, LANES), f32), V((rws, 1, LANES), f32),
        D((block_map.shape[0] + 1,)), D((6,)), D((2,)), D((6,)),
        D((n, rws)), D((n, rws)), D((n, cls)), D((n, cls)), D((n, cls)), D((n, cls)),
        D((n, rws)), D((n, rws)), D((n, CHUNKS, rws)), D((n, CHUNKS, rws)),
        D((n, CHUNKS, rws)), D((n, CHUNKS, rws)), D((rws,)), D((rws,)),
        D((n - 1, 2 * tms)), D((n - 1, 2 * tms)), D((n - 1, groups * rws)), D((n - 1, groups * rws)),
        D((cls,)), D((cls,)), D((rws,)), D((rws,)),
    ]
    return pl.pallas_call(
        functools.partial(kernel, (tms, rws, cls)),
        out_shape=(
            jax.ShapeDtypeStruct((scen, cols), f32),
            jax.ShapeDtypeStruct((scen, rows), f32),
            jax.ShapeDtypeStruct((1, 3, scen), f32),
        ),
        in_specs=[hbm] * 8,
        out_specs=(hbm, hbm, vmem),
        scratch_shapes=scratch,
        compiler_params=pltpu.CompilerParams(
            collective_id=0, has_side_effects=True, vmem_limit_bytes=63 << 20
        ),
        name="pdhg",
    )(
        matrix_tiles, block_map, link_tiles, demand, objective.reshape(1, cols), upper_bound.reshape(1, cols),
        restart_flag, step_index,
    )


def solution(mesh):
    in_specs = (
        P(("tm", "row"), "col"),
        P(("tm", "row"), "col"),
        P(("tm", "row"), "col"),
        P(None, ("tm", "row")),
        P(("tm", "col")),
        P(("tm", "col")),
        P(),
        P(),
    )
    out_specs = (P(None, ("tm", "col")), P(None, ("tm", "row")), P("tm", None, None))
    return jax.shard_map(
        on_device, mesh=mesh, in_specs=in_specs, out_specs=out_specs, check_vma=False
    )
```

```python
import functools

import jax
import jax.numpy as jnp
from jax import lax
from jax.experimental import pallas as pl
from jax.experimental.pallas import tpu as pltpu
from jax.sharding import PartitionSpec as P

ITERS = 3
CHUNKS = 4
LANES = 128
GROUP = 8
MESH = pl.DeviceIdType.MESH
NN = (((1,), (0,)), ((), ()))
NT = (((1,), (1,)), ((), ()))


def halves(x):
    high = x.astype(jnp.bfloat16)
    return high, (x - high.astype(jnp.float32)).astype(jnp.bfloat16)


def dot(a, b, dims):
    return lax.dot_general(a, b, dims, preferred_element_type=jnp.float32)


def product(left, high, low, dims):
    rows = left.shape[0] // 2
    both = dot(left, high, dims)
    return both[:rows] + (both[rows:] + dot(left[:rows], low, dims))


def stacked(x):
    return jnp.concatenate(halves(x), axis=0)


def column(row, start, size):
    shape = (size, row.shape[1])
    lane = lax.broadcasted_iota(jnp.int32, shape, 1)
    sub = lax.broadcasted_iota(jnp.int32, shape, 0)
    return jnp.sum(jnp.where(lane == sub + start, row, 0.0), axis=1, keepdims=True)


def spread(col, start):
    shape = (col.shape[0], LANES)
    lane = lax.broadcasted_iota(jnp.int32, shape, 1)
    sub = lax.broadcasted_iota(jnp.int32, shape, 0)
    return jnp.sum(jnp.where(lane == sub + start, col, 0.0), axis=0, keepdims=True)


def kernel(
    sizes,
    mat, bmap_in, link, dem_in, obj_in, ub_in, flags_in, steps_in,
    primal_out, dual_out, kkt_out,
    bmap, flags, steps, dem, costs, far,
    kf, lf, kh, kl, lh, ll,
    ybuf, ypiece, halo, pq, qb, wbuf, pa, side, ab, sb, zbuf, zpiece,
    xs, xavg, xanc, ds, davg, danc, qx, qavg,
    nsend, near_buf, wide_buf, fpart, fsum, fall,
    load_sem, small_sem, out_sem, pair_sem, hello,
    halo_s, halo_r, rsc_s, rsc_r, agc_s, agc_r,
    side_s, side_r, rsr_s, rsr_r, agr_s, agr_r, z_sem,
    near_s, near_r, wide_s, wide_r, fall_sem,
):
    tms, rws, cls = sizes
    rows, cols = kf.shape
    stor = lf.shape[1]
    edge = cols - stor
    scen = ybuf.shape[1]
    chunk = cols // CHUNKS
    half = rows // 2
    groups = scen // GROUP
    blk = rows // bmap.shape[0]
    t, r, c = lax.axis_index("tm"), lax.axis_index("row"), lax.axis_index("col")
    g, h = lax.div(c, 2), lax.rem(c, 2)
    o = lax.rem(t + tms // 2, tms)
    own_r = pl.multiple_of(r * GROUP, GROUP)
    own_g = pl.multiple_of(g * GROUP, GROUP)
    own_h = pl.multiple_of(h * half, half)
    near_first = (0, 1, 3, 2)
    far_first = near_first[::-1]
    order = [CHUNKS - 1] + list(range(CHUNKS - 1))

    def rem(a, n):
        return lax.rem(a, n)

    def at(tm=None, row=None, col=None):
        return {"tm": t if tm is None else tm, "row": r if row is None else row, "col": c if col is None else col}

    def descriptor(src, dst, ssem, rsem, where):
        return pltpu.make_async_remote_copy(
            src_ref=src, dst_ref=dst, send_sem=ssem, recv_sem=rsem, device_id=where, device_id_type=MESH
        )

    def send(src, dst, ssem, rsem, where):
        descriptor(src, dst, ssem, rsem, where).start()

    def arrived(whole, sem):
        descriptor(whole, whole, sem, sem, at()).wait_recv()

    def left(whole, sem):
        descriptor(whole, whole, sem, sem, at()).wait_send()

    small = [
        pltpu.make_async_copy(src, dst, small_sem.at[i])
        for i, (src, dst) in enumerate(
            (
                (steps_in, steps), (obj_in, costs.at[0]), (ub_in, costs.at[1]), (bmap_in, bmap), (flags_in, flags),
                (dem_in.at[pl.ds(own_g, GROUP), pl.ds(own_h, half)], dem),
            )
        )
    ]
    loads = []
    for i in range(rows // blk):
        part = pl.ds(i * blk, blk)
        loads.append(pltpu.make_async_copy(mat.at[part], kf.at[part], load_sem.at[i]))
    loads.append(pltpu.make_async_copy(link, lf, load_sem.at[rows // blk]))
    for copy in small + loads:
        copy.start()

    def near_peers():
        for dt in range(tms):
            for f in range(2):
                if dt or f:
                    yield dt * 2 + f, at(tm=rem(t + dt, tms), col=g * 2 + (1 - h if f else h))

    def wide_peers():
        for dr in (2, 1, 3, 0):
            for dg in range(groups):
                if dr or dg:
                    yield dr * groups + dg, at(row=rem(r + dr, rws), col=rem(g + dg, groups) * 2 + h)

    behind, ahead = rem(o + tms - 1, tms), rem(o + 1, tms)
    barrier = pltpu.get_barrier_semaphore()
    peers = [at(row=rem(r + d, rws)) for d in (2, 1, 3)]
    peers += [at(tm=rem(t + d, tms)) for d in range(1, tms)]
    peers += [at(col=rem(c + d, cls)) for d in range(1, cls)]
    for peer in peers:
        pl.semaphore_signal(barrier, inc=1, device_id=peer, device_id_type=MESH)

    weight = jnp.ones((1, scen), jnp.float32)
    count = jnp.zeros((1, scen), jnp.float32)

    def plan(k):
        eta = 0.15 * (1.0 + steps[k : k + 1, :].astype(jnp.float32))
        flag = flags[k : k + 1, :].astype(jnp.float32)
        return eta, flag

    def col_slots():
        for f in (1, 0):
            for dg in range(groups):
                if f == 0 and dg == 0:
                    continue
                hh = h if f == 0 else 1 - h
                yield dg * 2 + f, rem(g + dg, groups), hh, rem(g + groups - dg, groups)

    def send_rows_half(k, f):
        for slot, to_g, hh, _ in col_slots():
            if slot % 2 != f:
                continue
            src = pq.at[k, pl.ds(pl.multiple_of(to_g * GROUP, GROUP), GROUP), pl.ds(pl.multiple_of(hh * half, half), half)]
            send(src, qb.at[k, slot], rsc_s.at[k], rsc_r.at[k], at(col=to_g * 2 + hh))

    def receive_rows(k):
        total = pq[k, pl.ds(own_g, GROUP), pl.ds(own_h, half)]
        arrived(qb.at[k, pl.ds(1, cls - 1)], rsc_r.at[k])
        for slot in range(1, cls):
            total = total + qb[k, slot]
        return total

    def dual_step(k, weight, count, eta, flag):
        sigma = column(eta * weight, own_g, GROUP)
        cnt = column(count, own_g, GROUP)
        flg = column(flag, own_g, GROUP) > 0.5
        q = receive_rows(k)
        mine = dem[...]
        if k == 0:
            nxt = jnp.maximum(sigma * (mine - 2.0 * q), 0.0)
            avg, qa = nxt, q
            dual = nxt
            anchor = jnp.zeros_like(nxt)
        else:
            nxt = jnp.maximum(ds[...] + sigma * (mine - (2.0 * q - qx[...])), 0.0)
            avg = davg[...] + (nxt - davg[...]) / cnt
            qa = qavg[...] + (q - qavg[...]) / cnt
            dual = jnp.where(flg, avg, nxt)
            anchor = danc[...]
        ds[...] = dual
        wbuf[k, pl.ds(own_g, GROUP), pl.ds(own_h, half)] = dual
        piece = wbuf.at[k, pl.ds(own_g, GROUP), pl.ds(own_h, half)]
        for slot, to_g, hh, _ in col_slots():
            send(piece, piece, agc_s.at[k], agc_r.at[k], at(col=to_g * 2 + hh))
        davg[...] = avg
        qavg[...] = qa
        q_now = jnp.where(flg, qa, q)
        qx[...] = q_now
        dist = jnp.sum(jnp.square(avg - anchor), axis=1, keepdims=True)
        danc[...] = jnp.where(flg, avg, anchor)
        if k < ITERS - 1:
            return dist
        violation = jnp.sum(jnp.square(jnp.maximum(mine - q_now, 0.0)), axis=1, keepdims=True)
        return violation, jnp.sum(mine * dual, axis=1, keepdims=True)

    def adjoint_side(k, left):
        side[k] = product(left, lh[...], ll[...], NN)
        for d in range(rws):
            to_r = rem(r + d, rws)
            src = side.at[k, pl.ds(pl.multiple_of(to_r * GROUP, GROUP), GROUP)]
            send(src, sb.at[k, d], side_s.at[k], side_r.at[k], at(tm=behind, row=to_r))

    def adjoint_chunk(k, j, left):
        part = pl.ds(j * chunk, chunk)
        pa[k, :, part] = product(left, kh[:, part], kl[:, part], NN)
        for d in far_first:
            to_r = rem(r + d, rws)
            src = pa.at[k, pl.ds(pl.multiple_of(to_r * GROUP, GROUP), GROUP), part]
            send(src, ab.at[k, d, :, part], rsr_s.at[k], rsr_r.at[k, j], at(tm=o, row=to_r))

    def receive_adjoint(k, j):
        part = pl.ds(j * chunk, chunk)
        arrived(ab.at[k, :, :, part], rsr_r.at[k, j])
        total = (ab[k, 0, :, part] + ab[k, 1, :, part]) + (ab[k, 2, :, part] + ab[k, 3, :, part])
        if j == CHUNKS - 1:
            arrived(sb.at[k], side_r.at[k])
            extra = (sb[k, 0] + sb[k, 1]) + (sb[k, 2] + sb[k, 3])
            total = jnp.concatenate([total[:, : chunk - stor], total[:, chunk - stor :] + extra], axis=1)
        return total

    def primal_steps(k, weight, eta):
        tau = column(eta / weight, own_r, GROUP)
        for j in order:
            part = pl.ds(j * chunk, chunk)
            reduced = far[0, :, part] - receive_adjoint(k - 1, j)
            ypiece[k, :, part] = jnp.clip(xs[:, part] - tau * reduced, 0.0, far[1, :, part])
            for d in far_first:
                send(
                    ypiece.at[k, :, part], ybuf.at[k, pl.ds(own_r, GROUP), part],
                    agr_s.at[k], agr_r.at[k, j], at(tm=o, row=rem(r + d, rws)),
                )
            if j == CHUNKS - 1:
                for d in far_first:
                    send(
                        ypiece.at[k, :, pl.ds(edge, stor)], halo.at[k, pl.ds(own_r, GROUP)],
                        halo_s.at[k], halo_r.at[k], at(tm=ahead, row=rem(r + d, rws)),
                    )

    def primal_rest(k, count, flag):
        cnt = column(count, own_r, GROUP)
        flg = column(flag, own_r, GROUP) > 0.5
        nxt = ypiece[k]
        if k == 0:
            avg = nxt
            anchor = jnp.zeros_like(nxt)
        else:
            avg = xavg[...] + (nxt - xavg[...]) / cnt
            anchor = xanc[...]
        now = jnp.where(flg, avg, nxt)
        xs[...] = now
        xavg[...] = avg
        dist = jnp.sum(jnp.square(avg - anchor), axis=1, keepdims=True)
        xanc[...] = jnp.where(flg, avg, anchor)
        if k < ITERS - 1:
            return dist
        zpiece[...] = now
        for d in far_first:
            send(zpiece, zbuf.at[pl.ds(own_r, GROUP)], z_sem.at[0], z_sem.at[1], at(tm=o, row=rem(r + d, rws)))
        return jnp.sum(far[0] * now, axis=1, keepdims=True)

    def apply_chunks(k):
        acc = None
        for j in order:
            part = pl.ds(j * chunk, chunk)
            arrived(ybuf.at[k, :, part], agr_r.at[k, j])
            left = stacked(ybuf[k, :, part])
            if j != order[-1]:
                term = product(left, kh[:, part], kl[:, part], NT)
                if j == CHUNKS - 1:
                    arrived(halo.at[k], halo_r.at[k])
                    pq[k] = term + product(stacked(halo[k]), lh[...], ll[...], NT)
                else:
                    pq[k] = pq[k] + term
            else:
                for f in (1, 0):
                    hh = pl.multiple_of((h if f == 0 else 1 - h) * half, half)
                    some = pl.ds(hh, half)
                    pq[k, :, some] = pq[k, :, some] + product(left, kh[some, part], kl[some, part], NT)
                    send_rows_half(k, f)

    def norm_start(k, dx, dy):
        nsend[k, 0] = spread(dx, own_r) + spread(dy, scen + own_g)
        for slot, place in near_peers():
            send(nsend.at[k, 0], near_buf.at[k, slot], near_s.at[k], near_r.at[k], place)

    def norm_middle(k):
        total = nsend[k, 0]
        arrived(near_buf.at[k, pl.ds(1, 2 * tms - 1)], near_r.at[k])
        for slot, _ in near_peers():
            total = total + near_buf[k, slot]
        nsend[k, 1] = total
        for slot, place in wide_peers():
            send(nsend.at[k, 1], wide_buf.at[k, slot], wide_s.at[k], wide_r.at[k], place)

    def norm_weight(k, weight, flag):
        total = nsend[k, 1]
        arrived(wide_buf.at[k, pl.ds(1, groups * rws - 1)], wide_r.at[k])
        for slot, _ in wide_peers():
            total = total + wide_buf[k, slot]
        dx, dy = total[:, 0:scen], total[:, scen : 2 * scen]
        candidate = jnp.sqrt((dy + 1e-06) / (dx + 1e-06))
        return jnp.where(flag > 0.5, jnp.sqrt(weight * candidate), weight)

    for copy in small:
        copy.wait()
    eta, flag = plan(0)
    count = count + 1.0
    ybuf[0] = jnp.clip(-column(eta, 0, scen) * costs[0], 0.0, costs[1])
    left0 = stacked(ybuf[0])
    for i in range(rows // blk):
        loads[i].wait()
        part = pl.ds(i * blk, blk)
        for j in range(cols // blk):
            across = pl.ds(j * blk, blk)
            high, low = halves(kf[part, across] * bmap[i, j].astype(jnp.float32))
            kh[part, across] = high
            kl[part, across] = low
        pq[0, :, part] = product(left0, kh[part, :], kl[part, :], NT)
        if i == 1:
            pl.semaphore_wait(barrier, len(peers))
            send(ybuf.at[0, :, pl.ds(edge, stor)], halo.at[0], pair_sem.at[0], pair_sem.at[1], at(tm=rem(t + 1, tms)))
            send(costs, far, pair_sem.at[2], pair_sem.at[3], at(tm=o))
            for x in (behind, ahead):
                pl.semaphore_signal(hello, inc=1, device_id=at(tm=x), device_id_type=MESH)
    loads[-1].wait()
    high, low = halves(lf[...])
    lh[...] = high
    ll[...] = low
    arrived(halo.at[0], pair_sem.at[1])
    left0 = stacked(halo[0])
    for f in (1, 0):
        some = pl.ds(pl.multiple_of((h if f == 0 else 1 - h) * half, half), half)
        pq[0, :, some] = pq[0, :, some] + product(left0, lh[some, :], ll[some, :], NT)
        send_rows_half(0, f)
    arrived(far, pair_sem.at[3])
    pl.semaphore_wait(hello, 2)
    ypiece[0] = jnp.clip(-column(eta, own_r, GROUP) * far[0], 0.0, far[1])
    dx = primal_rest(0, count, flag)

    for k in range(ITERS):
        if k > 0:
            eta, flag = plan(k)
            count = count + 1.0
            primal_steps(k, weight, eta)
            dx = primal_rest(k, count, flag)
            apply_chunks(k)
        if k < ITERS - 1:
            dy = dual_step(k, weight, count, eta, flag)
            norm_start(k, dx, dy)
        else:
            viol, dual_part = dual_step(k, weight, count, eta, flag)
            fpart[0] = spread(viol, own_g) + spread(dual_part, scen + own_g)
            send(fpart.at[0], fpart.at[1], pair_sem.at[4], pair_sem.at[5], at(tm=o))
        arrived(qb.at[k, pl.ds(1, cls - 1)], agc_r.at[k])
        dual_parts = stacked(wbuf[k])
        adjoint_side(k, dual_parts)
        for n, j in enumerate(order):
            adjoint_chunk(k, j, dual_parts)
            if k < ITERS - 1 and n == 0:
                norm_middle(k)
        if k < ITERS - 1:
            weight = norm_weight(k, weight, flag)
            count = jnp.where(flag > 0.5, 0.0, count)

    k = ITERS - 1
    dual_copy = pltpu.make_async_copy(wbuf.at[k], dual_out, out_sem.at[0])
    dual_copy.start()
    arrived(zbuf, z_sem.at[1])
    primal_copy = pltpu.make_async_copy(zbuf, primal_out, out_sem.at[1])
    primal_copy.start()
    arrived(fpart.at[1], pair_sem.at[5])
    fixed = fpart[1] + spread(dx, 2 * scen + own_r)
    bound = jnp.zeros((GROUP, 1), jnp.float32)
    for j in order:
        part = pl.ds(j * chunk, chunk)
        reduced = far[0, :, part] - receive_adjoint(k, j)
        bound = bound + jnp.sum(far[1, :, part] * jnp.minimum(reduced, 0.0), axis=1, keepdims=True)
    fsum[...] = fixed + spread(bound, 3 * scen + own_r)
    for dr in far_first:
        for dc in (4, 3, 5, 2, 6, 1, 7, 0):
            place = at(tm=o, row=rem(r + dr, rws), col=rem(c + dc, cls))
            send(fsum, fall.at[r * cls + c], fall_sem.at[0], fall_sem.at[1], place)
    left(halo.at[0], pair_sem.at[0])
    left(costs, pair_sem.at[2])
    left(fpart.at[0], pair_sem.at[4])
    left(zbuf, z_sem.at[0])
    for k in range(ITERS):
        left(qb.at[k, pl.ds(1, cls - 1)], rsc_s.at[k])
        left(qb.at[k, pl.ds(1, cls - 1)], agc_s.at[k])
        left(side.at[k], side_s.at[k])
        left(pa.at[k], rsr_s.at[k])
        if k > 0:
            left(ybuf.at[k], agr_s.at[k])
            left(halo.at[k], halo_s.at[k])
        if k < ITERS - 1:
            left(near_buf.at[k, pl.ds(1, 2 * tms - 1)], near_s.at[k])
            left(wide_buf.at[k, pl.ds(1, groups * rws - 1)], wide_s.at[k])
    left(fall, fall_sem.at[0])
    dual_copy.wait()
    primal_copy.wait()
    arrived(fall, fall_sem.at[1])
    total = fall[0]
    for i in range(1, rws * cls):
        total = total + fall[i]
    con_total, var_total = float(rows * rws), float(cols * cls)
    parts = [total[:, i * scen : (i + 1) * scen] for i in range(4)]
    kkt_out[0, 0:1, :] = jnp.sqrt(parts[0] / con_total + 1e-06)
    kkt_out[0, 1:2, :] = parts[2] / var_total
    kkt_out[0, 2:3, :] = (parts[1] + parts[3]) / var_total


def on_device(matrix_tiles, block_map, link_tiles, demand, objective, upper_bound, restart_flag, step_index):
    rows, cols = matrix_tiles.shape
    stor = link_tiles.shape[1]
    scen = demand.shape[0]
    tms, rws, cls = lax.axis_size("tm"), lax.axis_size("row"), lax.axis_size("col")
    half = rows // 2
    groups = scen // GROUP
    f32, bf16 = jnp.float32, jnp.bfloat16
    vmem = pl.BlockSpec(memory_space=pltpu.VMEM)
    hbm = pl.BlockSpec(memory_space=pltpu.HBM)
    V = pltpu.VMEM
    D = pltpu.SemaphoreType.DMA
    n = ITERS
    scratch = [
        pltpu.SMEM(block_map.shape, jnp.int32), V(restart_flag.shape, jnp.int32), V(step_index.shape, jnp.int32),
        V((GROUP, half), f32), V((2, 1, cols), f32), V((2, 1, cols), f32),
        V((rows, cols), f32), V((rows, stor), f32),
        V((rows, cols), bf16), V((rows, cols), bf16), V((rows, stor), bf16), V((rows, stor), bf16),
        V((n, scen, cols), f32), V((n, GROUP, cols), f32), V((n, scen, stor), f32), V((n, scen, rows), f32),
        V((n, cls, GROUP, half), f32),
        V((n, scen, rows), f32), V((n, scen, cols), f32), V((n, scen, stor), f32),
        V((n, rws, GROUP, cols), f32), V((n, rws, GROUP, stor), f32), V((scen, cols), f32), V((GROUP, cols), f32),
        V((GROUP, cols), f32), V((GROUP, cols), f32), V((GROUP, cols), f32),
        V((GROUP, half), f32), V((GROUP, half), f32), V((GROUP, half), f32), V((GROUP, half), f32), V((GROUP, half), f32),
        V((n - 1, 2, 1, LANES), f32), V((n - 1, 2 * tms, 1, LANES), f32), V((n - 1, groups * rws, 1, LANES), f32),
        V((2, 1, LANES), f32), V((1, LANES), f32), V((rws * cls, 1, LANES), f32),
        D((block_map.shape[0] + 1,)), D((6,)), D((2,)), D((6,)), pltpu.SemaphoreType.REGULAR,
        D((n,)), D((n,)), D((n,)), D((n,)), D((n,)), D((n,)),
        D((n,)), D((n,)), D((n,)), D((n, CHUNKS)), D((n,)), D((n, CHUNKS)), D((2,)),
        D((n - 1,)), D((n - 1,)), D((n - 1,)), D((n - 1,)), D((2,)),
    ]
    return pl.pallas_call(
        functools.partial(kernel, (tms, rws, cls)),
        out_shape=(
            jax.ShapeDtypeStruct((scen, cols), f32),
            jax.ShapeDtypeStruct((scen, rows), f32),
            jax.ShapeDtypeStruct((1, 3, scen), f32),
        ),
        in_specs=[hbm] * 8,
        out_specs=(hbm, hbm, vmem),
        scratch_shapes=scratch,
        compiler_params=pltpu.CompilerParams(
            collective_id=0, has_side_effects=True, vmem_limit_bytes=48 << 20
        ),
        name="pdhg",
    )(*(
        pltpu.with_memory_space_constraint(x, pltpu.HBM)
        for x in (
            matrix_tiles, block_map, link_tiles, demand, objective.reshape(1, cols), upper_bound.reshape(1, cols),
            restart_flag, step_index,
        )
    ))


def solution(mesh):
    in_specs = (
        P(("tm", "row"), "col"),
        P(("tm", "row"), "col"),
        P(("tm", "row"), "col"),
        P(None, ("tm", "row")),
        P(("tm", "col")),
        P(("tm", "col")),
        P(),
        P(),
    )
    out_specs = (P(None, ("tm", "col")), P(None, ("tm", "row")), P("tm", None, None))
    return jax.shard_map(
        on_device, mesh=mesh, in_specs=in_specs, out_specs=out_specs, check_vma=False
    )
```

```python
import functools

import jax
import jax.numpy as jnp
from jax import lax
from jax.experimental import pallas as pl
from jax.experimental.pallas import tpu as pltpu
from jax.sharding import PartitionSpec as P

ITERS = 3
CHUNKS = ((0, 256), (1792, 256), (256, 512), (768, 512), (1280, 512))
LANES = 128
GROUP = 8
MESH = pl.DeviceIdType.MESH
NN = (((1,), (0,)), ((), ()))
NT = (((1,), (1,)), ((), ()))


def halves(x):
    high = x.astype(jnp.bfloat16)
    return high, (x - high.astype(jnp.float32)).astype(jnp.bfloat16)


def dot(a, b, dims):
    return lax.dot_general(a, b, dims, preferred_element_type=jnp.float32)


def product(left, high, low, dims):
    rows = left.shape[0] // 2
    both = dot(left, high, dims)
    return both[:rows] + (both[rows:] + dot(left[:rows], low, dims))


def stacked(x):
    return jnp.concatenate(halves(x), axis=0)


def column(row, start, size):
    shape = (size, row.shape[1])
    lane = lax.broadcasted_iota(jnp.int32, shape, 1)
    sub = lax.broadcasted_iota(jnp.int32, shape, 0)
    return jnp.sum(jnp.where(lane == sub + start, row, 0.0), axis=1, keepdims=True)


def spread(col, start):
    shape = (col.shape[0], LANES)
    lane = lax.broadcasted_iota(jnp.int32, shape, 1)
    sub = lax.broadcasted_iota(jnp.int32, shape, 0)
    return jnp.sum(jnp.where(lane == sub + start, col, 0.0), axis=0, keepdims=True)


def kernel(
    sizes,
    mat, bmap_in, link, dem_in, obj_in, ub_in, flags_in, steps_in,
    primal_out, dual_out, kkt_out,
    bmap, flags, steps, dem, costs, far,
    kf, lf, kh, kl, lh, ll,
    ybuf, gsum, gbuf, halo, pq, qb, wbuf, pa, side, ab, sb, zbuf,
    xs, xavg, xanc, ds, davg, danc, qx, qavg,
    near_buf, wide_buf, fpart, fsum, fall,
    load_sem, small_sem, out_sem, pair_sem, hello,
    halo_s, halo_r, rsc_s, rsc_r, agc_s, agc_r,
    side_s, side_r, rsr_s, rsr_r, agr_s, agr_r,
    near_s, near_r, wide_s, wide_r, fall_sem,
):
    tms, rws, cls = sizes
    rows, cols = kf.shape
    stor = lf.shape[1]
    edge = cols - stor
    scen = ybuf.shape[1]
    half = rows // 2
    groups = scen // GROUP
    blk = rows // bmap.shape[0]
    t, r, c = lax.axis_index("tm"), lax.axis_index("row"), lax.axis_index("col")
    g, h = lax.div(c, 2), lax.rem(c, 2)
    o = lax.rem(t + tms // 2, tms)
    own_r = pl.multiple_of(r * GROUP, GROUP)
    own_g = pl.multiple_of(g * GROUP, GROUP)
    own_h = pl.multiple_of(h * half, half)
    near_first = (0, 1, 3, 2)
    far_first = near_first[::-1]
    final = len(CHUNKS) - 1

    def rem(a, n):
        return lax.rem(a, n)

    def at(tm=None, row=None, col=None):
        return {"tm": t if tm is None else tm, "row": r if row is None else row, "col": c if col is None else col}

    def descriptor(src, dst, ssem, rsem, where):
        return pltpu.make_async_remote_copy(
            src_ref=src, dst_ref=dst, send_sem=ssem, recv_sem=rsem, device_id=where, device_id_type=MESH
        )

    def send(src, dst, ssem, rsem, where):
        descriptor(src, dst, ssem, rsem, where).start()

    def arrived(whole, sem):
        descriptor(whole, whole, sem, sem, at()).wait_recv()

    def left(whole, sem):
        descriptor(whole, whole, sem, sem, at()).wait_send()

    small = [
        pltpu.make_async_copy(src, dst, small_sem.at[i])
        for i, (src, dst) in enumerate(
            (
                (steps_in, steps), (obj_in, costs.at[0]), (ub_in, costs.at[1]), (bmap_in, bmap), (flags_in, flags),
                (dem_in.at[pl.ds(own_g, GROUP), pl.ds(own_h, half)], dem),
            )
        )
    ]
    loads = []
    for i in range(rows // blk):
        part = pl.ds(i * blk, blk)
        loads.append(pltpu.make_async_copy(mat.at[part], kf.at[part], load_sem.at[i]))
    loads.append(pltpu.make_async_copy(link, lf, load_sem.at[rows // blk]))
    for copy in small + loads:
        copy.start()

    def near_peers():
        for dt in range(tms):
            for f in range(2):
                if dt or f:
                    yield at(tm=rem(t + dt, tms), col=g * 2 + (1 - h if f else h))

    def wide_peers():
        for dr in (2, 1, 3, 0):
            for dg in range(groups):
                if dr or dg:
                    yield at(row=rem(r + dr, rws), col=rem(g + dg, groups) * 2 + h)

    behind, ahead = rem(o + tms - 1, tms), rem(o + 1, tms)
    barrier = pltpu.get_barrier_semaphore()
    peers = [at(row=rem(r + d, rws)) for d in (2, 1, 3)]
    peers += [at(tm=rem(t + d, tms)) for d in range(1, tms)]
    peers += [at(col=rem(c + d, cls)) for d in range(1, cls)]
    for peer in peers:
        pl.semaphore_signal(barrier, inc=1, device_id=peer, device_id_type=MESH)

    weight = jnp.ones((1, scen), jnp.float32)
    count = jnp.zeros((1, scen), jnp.float32)

    def plan(k):
        eta = 0.15 * (1.0 + steps[k : k + 1, :].astype(jnp.float32))
        flag = flags[k : k + 1, :].astype(jnp.float32)
        return eta, flag

    def col_slots():
        for f in (1, 0):
            for dg in range(groups):
                if f == 0 and dg == 0:
                    continue
                hh = h if f == 0 else 1 - h
                yield dg * 2 + f, rem(g + dg, groups), hh, rem(g + groups - dg, groups)

    def send_rows_half(k, f):
        for slot, to_g, hh, _ in col_slots():
            if slot % 2 != f:
                continue
            src = pq.at[k, pl.ds(pl.multiple_of(to_g * GROUP, GROUP), GROUP), pl.ds(pl.multiple_of(hh * half, half), half)]
            send(src, qb.at[k, slot], rsc_s.at[k], rsc_r.at[k], at(col=to_g * 2 + hh))

    def receive_rows(k):
        total = pq[k, pl.ds(own_g, GROUP), pl.ds(own_h, half)]
        arrived(qb.at[k, pl.ds(1, cls - 1)], rsc_r.at[k])
        for slot in range(1, cls):
            total = total + qb[k, slot]
        return total

    def dual_step(k, weight, count, eta, flag):
        sigma = column(eta * weight, own_g, GROUP)
        cnt = column(count, own_g, GROUP)
        flg = column(flag, own_g, GROUP) > 0.5
        q = receive_rows(k)
        mine = dem[...]
        if k == 0:
            nxt = jnp.maximum(sigma * (mine - 2.0 * q), 0.0)
            avg, qa = nxt, q
            dual = nxt
            anchor = jnp.zeros_like(nxt)
        else:
            nxt = jnp.maximum(ds[...] + sigma * (mine - (2.0 * q - qx[...])), 0.0)
            avg = davg[...] + (nxt - davg[...]) / cnt
            qa = qavg[...] + (q - qavg[...]) / cnt
            dual = jnp.where(flg, avg, nxt)
            anchor = danc[...]
        ds[...] = dual
        wbuf[k, pl.ds(own_g, GROUP), pl.ds(own_h, half)] = dual
        piece = wbuf.at[k, pl.ds(own_g, GROUP), pl.ds(own_h, half)]
        for slot, to_g, hh, _ in col_slots():
            send(piece, piece, agc_s.at[k], agc_r.at[k], at(col=to_g * 2 + hh))
        davg[...] = avg
        qavg[...] = qa
        q_now = jnp.where(flg, qa, q)
        qx[...] = q_now
        dist = jnp.sum(jnp.square(avg - anchor), axis=1, keepdims=True)
        danc[...] = jnp.where(flg, avg, anchor)
        if k < ITERS - 1:
            return dist
        violation = jnp.sum(jnp.square(jnp.maximum(mine - q_now, 0.0)), axis=1, keepdims=True)
        return violation, jnp.sum(mine * dual, axis=1, keepdims=True)

    def adjoint_side(k, left):
        side[k] = product(left, lh[...], ll[...], NN)
        for d in range(rws):
            to_r = rem(r + d, rws)
            src = side.at[k, pl.ds(pl.multiple_of(to_r * GROUP, GROUP), GROUP)]
            send(src, sb.at[k, d], side_s.at[k], side_r.at[k], at(tm=behind, row=to_r))

    def adjoint_chunk(k, j, left):
        part = pl.ds(*CHUNKS[j])
        pa[k, :, part] = product(left, kh[:, part], kl[:, part], NN)
        for d in far_first:
            to_r = rem(r + d, rws)
            src = pa.at[k, pl.ds(pl.multiple_of(to_r * GROUP, GROUP), GROUP), part]
            send(src, ab.at[k, d, :, part], rsr_s.at[k], rsr_r.at[k, j], at(tm=o, row=to_r))

    def receive_adjoint(k, j):
        part = pl.ds(*CHUNKS[j])
        arrived(ab.at[k, :, :, part], rsr_r.at[k, j])
        total = (ab[k, 0, :, part] + ab[k, 1, :, part]) + (ab[k, 2, :, part] + ab[k, 3, :, part])
        if CHUNKS[j][0] == edge:
            arrived(sb.at[k], side_r.at[k])
            extra = (sb[k, 0] + sb[k, 1]) + (sb[k, 2] + sb[k, 3])
            total = total + extra
        return total

    def adjoint_sums(k):
        for j in range(len(CHUNKS)):
            part = pl.ds(*CHUNKS[j])
            gsum[k, :, part] = receive_adjoint(k, j)
            for d in far_first:
                send(
                    gsum.at[k, :, part], gbuf.at[k, pl.ds(own_r, GROUP), part],
                    agr_s.at[k], agr_r.at[k, j], at(tm=o, row=rem(r + d, rws)),
                )

    def primal_rest(k, count, flag):
        cnt = column(count, 0, scen)
        flg = column(flag, 0, scen) > 0.5
        mine = pl.ds(own_r, GROUP)
        for first, size in CHUNKS:
            part = pl.ds(first, size)
            nxt = ybuf[k, :, part]
            avg = nxt if k == 0 else xavg[:, part] + (nxt - xavg[:, part]) / cnt
            xavg[:, part] = avg
            now = jnp.where(flg, avg, nxt)
            if k < ITERS - 1:
                xs[:, part] = now
            else:
                zbuf[:, part] = now
        if k == ITERS - 1:
            return jnp.sum(costs[0] * zbuf[mine, :], axis=1, keepdims=True)
        avg = xavg[mine, :]
        anchor = jnp.zeros_like(avg) if k == 0 else xanc[...]
        xanc[...] = jnp.where(column(flag, own_r, GROUP) > 0.5, avg, anchor)
        return jnp.sum(jnp.square(avg - anchor), axis=1, keepdims=True)

    def apply_chunks(k, tau):
        for j in range(len(CHUNKS)):
            part = pl.ds(*CHUNKS[j])
            arrived(gbuf.at[k - 1, :, part], agr_r.at[k - 1, j])
            reduced = costs[0, :, part] - gbuf[k - 1, :, part]
            nxt = jnp.clip(xs[:, part] - tau * reduced, 0.0, costs[1, :, part])
            ybuf[k, :, part] = nxt
            left = stacked(nxt)
            if CHUNKS[j][0] == edge:
                send(ybuf.at[k, :, part], halo.at[k], halo_s.at[k], halo_r.at[k], at(tm=rem(t + 1, tms)))
            if j != final:
                term = product(left, kh[:, part], kl[:, part], NT)
                if j == final - 1:
                    arrived(halo.at[k], halo_r.at[k])
                    term = term + product(stacked(halo[k]), lh[...], ll[...], NT)
                pq[k] = term if j == 0 else pq[k] + term
            else:
                for f in (1, 0):
                    hh = pl.multiple_of((h if f == 0 else 1 - h) * half, half)
                    some = pl.ds(hh, half)
                    pq[k, :, some] = pq[k, :, some] + product(left, kh[some, part], kl[some, part], NT)
                    send_rows_half(k, f)

    def norm_start(k, dx, dy):
        place = t * 2 + h
        near_buf[k, place] = spread(dx, own_r) + spread(dy, scen + own_g)
        for peer in near_peers():
            send(near_buf.at[k, place], near_buf.at[k, place], near_s.at[k], near_r.at[k], peer)

    def norm_middle(k):
        arrived(near_buf.at[k, pl.ds(1, 2 * tms - 1)], near_r.at[k])
        total = near_buf[k, 0]
        for i in range(1, 2 * tms):
            total = total + near_buf[k, i]
        place = r * groups + g
        wide_buf[k, place] = total
        for peer in wide_peers():
            send(wide_buf.at[k, place], wide_buf.at[k, place], wide_s.at[k], wide_r.at[k], peer)

    def norm_weight(k, weight, flag):
        arrived(wide_buf.at[k, pl.ds(1, groups * rws - 1)], wide_r.at[k])
        total = wide_buf[k, 0]
        for i in range(1, groups * rws):
            total = total + wide_buf[k, i]
        dx, dy = total[:, 0:scen], total[:, scen : 2 * scen]
        candidate = jnp.sqrt((dy + 1e-06) / (dx + 1e-06))
        return jnp.where(flag > 0.5, jnp.sqrt(weight * candidate), weight)

    for copy in small:
        copy.wait()
    eta, flag = plan(0)
    count = count + 1.0
    ybuf[0] = jnp.clip(-column(eta, 0, scen) * costs[0], 0.0, costs[1])
    left0 = stacked(ybuf[0])
    for i in range(rows // blk):
        loads[i].wait()
        part = pl.ds(i * blk, blk)
        for j in range(cols // blk):
            across = pl.ds(j * blk, blk)
            high, low = halves(kf[part, across] * bmap[i, j].astype(jnp.float32))
            kh[part, across] = high
            kl[part, across] = low
        pq[0, :, part] = product(left0, kh[part, :], kl[part, :], NT)
        if i == 1:
            pl.semaphore_wait(barrier, len(peers))
            send(ybuf.at[0, :, pl.ds(edge, stor)], halo.at[0], pair_sem.at[0], pair_sem.at[1], at(tm=rem(t + 1, tms)))
            send(costs, far, pair_sem.at[2], pair_sem.at[3], at(tm=o))
            pl.semaphore_signal(hello, inc=1, device_id=at(tm=ahead), device_id_type=MESH)
    loads[-1].wait()
    high, low = halves(lf[...])
    lh[...] = high
    ll[...] = low
    arrived(halo.at[0], pair_sem.at[1])
    left0 = stacked(halo[0])
    for f in (1, 0):
        some = pl.ds(pl.multiple_of((h if f == 0 else 1 - h) * half, half), half)
        pq[0, :, some] = pq[0, :, some] + product(left0, lh[some, :], ll[some, :], NT)
        send_rows_half(0, f)
    arrived(far, pair_sem.at[3])
    pl.semaphore_wait(hello, 1)
    dx = primal_rest(0, count, flag)

    for k in range(ITERS):
        if k > 0:
            eta, flag = plan(k)
            count = count + 1.0
            apply_chunks(k, column(eta / weight, 0, scen))
            dx = primal_rest(k, count, flag)
            if k == ITERS - 1:
                primal_copy = pltpu.make_async_copy(zbuf, primal_out, out_sem.at[1])
                primal_copy.start()
        if k < ITERS - 1:
            dy = dual_step(k, weight, count, eta, flag)
            norm_start(k, dx, dy)
        else:
            viol, dual_part = dual_step(k, weight, count, eta, flag)
            fpart[0] = spread(viol, own_g) + spread(dual_part, scen + own_g) + spread(dx, 2 * scen + own_r)
            send(fpart.at[0], fpart.at[1], pair_sem.at[4], pair_sem.at[5], at(tm=o))
        arrived(qb.at[k, pl.ds(1, cls - 1)], agc_r.at[k])
        dual_parts = stacked(wbuf[k])
        for j in range(len(CHUNKS)):
            adjoint_chunk(k, j, dual_parts)
            if j == 0:
                adjoint_side(k, dual_parts)
                if k < ITERS - 1:
                    norm_middle(k)
        if k < ITERS - 1:
            adjoint_sums(k)
            weight = norm_weight(k, weight, flag)
            count = jnp.where(flag > 0.5, 0.0, count)

    k = ITERS - 1
    dual_copy = pltpu.make_async_copy(wbuf.at[k], dual_out, out_sem.at[0])
    dual_copy.start()
    arrived(fpart.at[1], pair_sem.at[5])
    bound = jnp.zeros((GROUP, 1), jnp.float32)
    for j in range(len(CHUNKS)):
        part = pl.ds(*CHUNKS[j])
        reduced = far[0, :, part] - receive_adjoint(k, j)
        bound = bound + jnp.sum(far[1, :, part] * jnp.minimum(reduced, 0.0), axis=1, keepdims=True)
    fsum[...] = fpart[1] + spread(bound, 3 * scen + own_r)
    for dr in far_first:
        for dc in (4, 3, 5, 2, 6, 1, 7, 0):
            place = at(tm=o, row=rem(r + dr, rws), col=rem(c + dc, cls))
            send(fsum, fall.at[r * cls + c], fall_sem.at[0], fall_sem.at[1], place)
    left(halo.at[0], pair_sem.at[0])
    left(costs, pair_sem.at[2])
    left(fpart.at[0], pair_sem.at[4])
    for k in range(ITERS):
        left(qb.at[k, pl.ds(1, cls - 1)], rsc_s.at[k])
        left(qb.at[k, pl.ds(1, cls - 1)], agc_s.at[k])
        left(side.at[k], side_s.at[k])
        left(pa.at[k], rsr_s.at[k])
        if k > 0:
            left(gbuf.at[k - 1], agr_s.at[k - 1])
            left(halo.at[k], halo_s.at[k])
        if k < ITERS - 1:
            left(near_buf.at[k, pl.ds(1, 2 * tms - 1)], near_s.at[k])
            left(wide_buf.at[k, pl.ds(1, groups * rws - 1)], wide_s.at[k])
    left(fall, fall_sem.at[0])
    dual_copy.wait()
    primal_copy.wait()
    arrived(fall, fall_sem.at[1])
    total = fall[0]
    for i in range(1, rws * cls):
        total = total + fall[i]
    con_total, var_total = float(rows * rws), float(cols * cls)
    parts = [total[:, i * scen : (i + 1) * scen] for i in range(4)]
    kkt_out[0, 0:1, :] = jnp.sqrt(parts[0] / con_total + 1e-06)
    kkt_out[0, 1:2, :] = parts[2] / var_total
    kkt_out[0, 2:3, :] = (parts[1] + parts[3]) / var_total


def on_device(matrix_tiles, block_map, link_tiles, demand, objective, upper_bound, restart_flag, step_index):
    rows, cols = matrix_tiles.shape
    stor = link_tiles.shape[1]
    scen = demand.shape[0]
    tms, rws, cls = lax.axis_size("tm"), lax.axis_size("row"), lax.axis_size("col")
    half = rows // 2
    groups = scen // GROUP
    f32, bf16 = jnp.float32, jnp.bfloat16
    vmem = pl.BlockSpec(memory_space=pltpu.VMEM)
    hbm = pl.BlockSpec(memory_space=pltpu.HBM)
    V = pltpu.VMEM
    D = pltpu.SemaphoreType.DMA
    n = ITERS
    scratch = [
        pltpu.SMEM(block_map.shape, jnp.int32), V(restart_flag.shape, jnp.int32), V(step_index.shape, jnp.int32),
        V((GROUP, half), f32), V((2, 1, cols), f32), V((2, 1, cols), f32),
        V((rows, cols), f32), V((rows, stor), f32),
        V((rows, cols), bf16), V((rows, cols), bf16), V((rows, stor), bf16), V((rows, stor), bf16),
        V((n, scen, cols), f32), V((n - 1, GROUP, cols), f32), V((n - 1, scen, cols), f32), V((n, scen, stor), f32), V((n, scen, rows), f32),
        V((n, cls, GROUP, half), f32),
        V((n, scen, rows), f32), V((n, scen, cols), f32), V((n, scen, stor), f32),
        V((n, rws, GROUP, cols), f32), V((n, rws, GROUP, stor), f32), V((scen, cols), f32),
        V((scen, cols), f32), V((scen, cols), f32), V((GROUP, cols), f32),
        V((GROUP, half), f32), V((GROUP, half), f32), V((GROUP, half), f32), V((GROUP, half), f32), V((GROUP, half), f32),
        V((n - 1, 2 * tms, 1, LANES), f32), V((n - 1, groups * rws, 1, LANES), f32),
        V((2, 1, LANES), f32), V((1, LANES), f32), V((rws * cls, 1, LANES), f32),
        D((block_map.shape[0] + 1,)), D((6,)), D((2,)), D((6,)), pltpu.SemaphoreType.REGULAR,
        D((n,)), D((n,)), D((n,)), D((n,)), D((n,)), D((n,)),
        D((n,)), D((n,)), D((n,)), D((n, len(CHUNKS))), D((n - 1,)), D((n - 1, len(CHUNKS))),
        D((n - 1,)), D((n - 1,)), D((n - 1,)), D((n - 1,)), D((2,)),
    ]
    return pl.pallas_call(
        functools.partial(kernel, (tms, rws, cls)),
        out_shape=(
            jax.ShapeDtypeStruct((scen, cols), f32),
            jax.ShapeDtypeStruct((scen, rows), f32),
            jax.ShapeDtypeStruct((1, 3, scen), f32),
        ),
        in_specs=[hbm] * 8,
        out_specs=(hbm, hbm, vmem),
        scratch_shapes=scratch,
        compiler_params=pltpu.CompilerParams(
            collective_id=0, has_side_effects=True, vmem_limit_bytes=48 << 20
        ),
        name="pdhg",
    )(*(
        pltpu.with_memory_space_constraint(x, pltpu.HBM)
        for x in (
            matrix_tiles, block_map, link_tiles, demand, objective.reshape(1, cols), upper_bound.reshape(1, cols),
            restart_flag, step_index,
        )
    ))


def solution(mesh):
    in_specs = (
        P(("tm", "row"), "col"),
        P(("tm", "row"), "col"),
        P(("tm", "row"), "col"),
        P(None, ("tm", "row")),
        P(("tm", "col")),
        P(("tm", "col")),
        P(),
        P(),
    )
    out_specs = (P(None, ("tm", "col")), P(None, ("tm", "row")), P("tm", None, None))
    return jax.shard_map(
        on_device, mesh=mesh, in_specs=in_specs, out_specs=out_specs, check_vma=False
    )
```

```python
import functools

import jax
import jax.numpy as jnp
from jax import lax
from jax.experimental import pallas as pl
from jax.experimental.pallas import tpu as pltpu
from jax.sharding import PartitionSpec as P

ITERS = 3
CHUNKS = ((0, 256), (1792, 256), (256, 512), (768, 512), (1280, 512))
LANES = 128
GROUP = 8
MESH = pl.DeviceIdType.MESH
NN = (((1,), (0,)), ((), ()))
NT = (((1,), (1,)), ((), ()))


def halves(x):
    high = x.astype(jnp.bfloat16)
    return high, (x - high.astype(jnp.float32)).astype(jnp.bfloat16)


def dot(a, b, dims):
    return lax.dot_general(a, b, dims, preferred_element_type=jnp.float32)


def product(left, high, low, dims):
    rows = left.shape[0] // 2
    both = dot(left, high, dims)
    return both[:rows] + (both[rows:] + dot(left[:rows], low, dims))


def stacked(x):
    return jnp.concatenate(halves(x), axis=0)


def column(row, start, size):
    shape = (size, row.shape[1])
    lane = lax.broadcasted_iota(jnp.int32, shape, 1)
    sub = lax.broadcasted_iota(jnp.int32, shape, 0)
    return jnp.sum(jnp.where(lane == sub + start, row, 0.0), axis=1, keepdims=True)


def spread(col, start):
    shape = (col.shape[0], LANES)
    lane = lax.broadcasted_iota(jnp.int32, shape, 1)
    sub = lax.broadcasted_iota(jnp.int32, shape, 0)
    return jnp.sum(jnp.where(lane == sub + start, col, 0.0), axis=0, keepdims=True)


def kernel(
    sizes,
    mat, bmap_in, link, dem_in, obj_in, ub_in, flags_in, steps_in,
    primal_out, dual_out, kkt_out,
    bmap, flags, steps, dem, costs, far,
    kf, lf, kh, kl, lh, ll,
    ybuf, gsum, gbuf, halo, pq, sib, ysum, wbuf, pa, side, ab, sb, zbuf,
    xs, xavg, xanc, ds, davg, danc, qx, qavg,
    near_buf, wide_buf, fpart, fsum, fall,
    load_sem, small_sem, out_sem, pair_sem, hello,
    halo_s, halo_r, sib_s, sib_r, y_s, y_r, dual_s, dual_r,
    side_s, side_r, rsr_s, rsr_r, agr_s, agr_r,
    near_s, near_r, wide_s, wide_r, fall_sem,
):
    tms, rws, cls = sizes
    rows, cols = kf.shape
    stor = lf.shape[1]
    edge = cols - stor
    scen = ybuf.shape[1]
    half = rows // 2
    groups = scen // GROUP
    blk = rows // bmap.shape[0]
    t, r, c = lax.axis_index("tm"), lax.axis_index("row"), lax.axis_index("col")
    g, h = lax.div(c, 2), lax.rem(c, 2)
    o = lax.rem(t + tms // 2, tms)
    own_r = pl.multiple_of(r * GROUP, GROUP)
    own_h = pl.ds(pl.multiple_of(h * half, half), half)
    other_h = pl.ds(pl.multiple_of((1 - h) * half, half), half)
    near_first = (0, 1, 3, 2)
    far_first = near_first[::-1]
    final = len(CHUNKS) - 1

    def rem(a, n):
        return lax.rem(a, n)

    def at(tm=None, row=None, col=None):
        return {"tm": t if tm is None else tm, "row": r if row is None else row, "col": c if col is None else col}

    def descriptor(src, dst, ssem, rsem, where):
        return pltpu.make_async_remote_copy(
            src_ref=src, dst_ref=dst, send_sem=ssem, recv_sem=rsem, device_id=where, device_id_type=MESH
        )

    def send(src, dst, ssem, rsem, where):
        descriptor(src, dst, ssem, rsem, where).start()

    def arrived(whole, sem):
        descriptor(whole, whole, sem, sem, at()).wait_recv()

    def left(whole, sem):
        descriptor(whole, whole, sem, sem, at()).wait_send()

    small = [
        pltpu.make_async_copy(src, dst, small_sem.at[i])
        for i, (src, dst) in enumerate(
            (
                (steps_in, steps), (obj_in, costs.at[0]), (ub_in, costs.at[1]), (bmap_in, bmap), (flags_in, flags),
                (dem_in.at[:, own_h], dem),
            )
        )
    ]
    loads = []
    for i in range(rows // blk):
        part = pl.ds(i * blk, blk)
        loads.append(pltpu.make_async_copy(mat.at[part], kf.at[part], load_sem.at[i]))
    loads.append(pltpu.make_async_copy(link, lf, load_sem.at[rows // blk]))
    for copy in small + loads:
        copy.start()

    def near_peers():
        for dt in range(tms):
            for f in range(2):
                if dt or f:
                    yield at(tm=rem(t + dt, tms), col=g * 2 + (1 - h if f else h))

    def wide_peers():
        for dr in (2, 1, 3, 0):
            for dg in range(groups):
                if dr or dg:
                    yield at(row=rem(r + dr, rws), col=rem(g + dg, groups) * 2 + h)

    behind, ahead = rem(o + tms - 1, tms), rem(o + 1, tms)
    barrier = pltpu.get_barrier_semaphore()
    peers = [at(row=rem(r + d, rws)) for d in (2, 1, 3)]
    peers += [at(tm=rem(t + d, tms)) for d in range(1, tms)]
    peers += [at(col=rem(c + d, cls)) for d in range(1, cls)]
    for peer in peers:
        pl.semaphore_signal(barrier, inc=1, device_id=peer, device_id_type=MESH)

    weight = jnp.ones((1, scen), jnp.float32)
    count = jnp.zeros((1, scen), jnp.float32)

    def plan(k):
        eta = 0.15 * (1.0 + steps[k : k + 1, :].astype(jnp.float32))
        flag = flags[k : k + 1, :].astype(jnp.float32)
        return eta, flag

    sibling = at(col=g * 2 + 1 - h)

    def sum_rows(k):
        arrived(sib.at[k], sib_r.at[k])
        ysum[k, g] = pq[k, :, own_h] + sib[k]
        for dg in (2, 1, 3):
            send(ysum.at[k, g], ysum.at[k, g], y_s.at[k], y_r.at[k], at(col=rem(g + dg, groups) * 2 + h))

    def dual_step(k, weight, count, eta, flag):
        sigma = column(eta * weight, 0, scen)
        cnt = column(count, 0, scen)
        flg = column(flag, 0, scen) > 0.5
        arrived(ysum.at[k, pl.ds(1, groups - 1)], y_r.at[k])
        q = ysum[k, 0]
        for i in range(1, groups):
            q = q + ysum[k, i]
        mine = dem[...]
        if k == 0:
            nxt = jnp.maximum(sigma * (mine - 2.0 * q), 0.0)
            avg, qa = nxt, q
            dual = nxt
            anchor = jnp.zeros_like(nxt)
        else:
            nxt = jnp.maximum(ds[...] + sigma * (mine - (2.0 * q - qx[...])), 0.0)
            avg = davg[...] + (nxt - davg[...]) / cnt
            qa = qavg[...] + (q - qavg[...]) / cnt
            dual = jnp.where(flg, avg, nxt)
            anchor = danc[...]
        ds[...] = dual
        wbuf[k, :, own_h] = dual
        send(wbuf.at[k, :, own_h], wbuf.at[k, :, own_h], dual_s.at[k], dual_r.at[k], sibling)
        davg[...] = avg
        qavg[...] = qa
        q_now = jnp.where(flg, qa, q)
        qx[...] = q_now
        dist = jnp.sum(jnp.square(avg - anchor), axis=1, keepdims=True)
        danc[...] = jnp.where(flg, avg, anchor)
        if k < ITERS - 1:
            return dist
        violation = jnp.sum(jnp.square(jnp.maximum(mine - q_now, 0.0)), axis=1, keepdims=True)
        return violation, jnp.sum(mine * dual, axis=1, keepdims=True)

    def adjoint_own(k):
        parts = stacked(wbuf[k, :, own_h])
        for first, size in CHUNKS:
            part = pl.ds(first, size)
            pa[k, :, part] = product(parts, kh[own_h, part], kl[own_h, part], NN)
        side[k] = product(parts, lh[own_h, :], ll[own_h, :], NN)

    def adjoint_side(k, left):
        side[k] = side[k] + product(left, lh[other_h, :], ll[other_h, :], NN)
        for d in range(rws):
            to_r = rem(r + d, rws)
            src = side.at[k, pl.ds(pl.multiple_of(to_r * GROUP, GROUP), GROUP)]
            send(src, sb.at[k, d], side_s.at[k], side_r.at[k], at(tm=behind, row=to_r))

    def adjoint_chunk(k, j, left):
        part = pl.ds(*CHUNKS[j])
        pa[k, :, part] = pa[k, :, part] + product(left, kh[other_h, part], kl[other_h, part], NN)
        for d in far_first:
            to_r = rem(r + d, rws)
            src = pa.at[k, pl.ds(pl.multiple_of(to_r * GROUP, GROUP), GROUP), part]
            send(src, ab.at[k, d, :, part], rsr_s.at[k], rsr_r.at[k, j], at(tm=o, row=to_r))

    def receive_adjoint(k, j):
        part = pl.ds(*CHUNKS[j])
        arrived(ab.at[k, :, :, part], rsr_r.at[k, j])
        total = (ab[k, 0, :, part] + ab[k, 1, :, part]) + (ab[k, 2, :, part] + ab[k, 3, :, part])
        if CHUNKS[j][0] == edge:
            arrived(sb.at[k], side_r.at[k])
            extra = (sb[k, 0] + sb[k, 1]) + (sb[k, 2] + sb[k, 3])
            total = total + extra
        return total

    def adjoint_sums(k):
        for j in range(len(CHUNKS)):
            part = pl.ds(*CHUNKS[j])
            gsum[k, :, part] = receive_adjoint(k, j)
            for d in far_first:
                send(
                    gsum.at[k, :, part], gbuf.at[k, pl.ds(own_r, GROUP), part],
                    agr_s.at[k], agr_r.at[k, j], at(tm=o, row=rem(r + d, rws)),
                )

    def primal_rest(k, count, flag):
        cnt = column(count, 0, scen)
        flg = column(flag, 0, scen) > 0.5
        mine = pl.ds(own_r, GROUP)
        for first, size in CHUNKS:
            part = pl.ds(first, size)
            nxt = ybuf[k, :, part]
            avg = nxt if k == 0 else xavg[:, part] + (nxt - xavg[:, part]) / cnt
            xavg[:, part] = avg
            now = jnp.where(flg, avg, nxt)
            if k < ITERS - 1:
                xs[:, part] = now
            else:
                zbuf[:, part] = now
        if k == ITERS - 1:
            return jnp.sum(costs[0] * zbuf[mine, :], axis=1, keepdims=True)
        avg = xavg[mine, :]
        anchor = jnp.zeros_like(avg) if k == 0 else xanc[...]
        xanc[...] = jnp.where(column(flag, own_r, GROUP) > 0.5, avg, anchor)
        return jnp.sum(jnp.square(avg - anchor), axis=1, keepdims=True)

    def apply_chunks(k, tau):
        for j in range(len(CHUNKS)):
            part = pl.ds(*CHUNKS[j])
            arrived(gbuf.at[k - 1, :, part], agr_r.at[k - 1, j])
            reduced = costs[0, :, part] - gbuf[k - 1, :, part]
            nxt = jnp.clip(xs[:, part] - tau * reduced, 0.0, costs[1, :, part])
            ybuf[k, :, part] = nxt
            left = stacked(nxt)
            if CHUNKS[j][0] == edge:
                send(ybuf.at[k, :, part], halo.at[k], halo_s.at[k], halo_r.at[k], at(tm=rem(t + 1, tms)))
            if j != final:
                term = product(left, kh[:, part], kl[:, part], NT)
                if j == final - 1:
                    arrived(halo.at[k], halo_r.at[k])
                    term = term + product(stacked(halo[k]), lh[...], ll[...], NT)
                pq[k] = term if j == 0 else pq[k] + term
            else:
                for some in (other_h, own_h):
                    pq[k, :, some] = pq[k, :, some] + product(left, kh[some, part], kl[some, part], NT)
                    if some is other_h:
                        send(pq.at[k, :, some], sib.at[k], sib_s.at[k], sib_r.at[k], sibling)

    def norm_start(k, dx, dy):
        place = t * 2 + h
        near_buf[k, place] = spread(dx, own_r) + spread(dy / groups, scen)
        for peer in near_peers():
            send(near_buf.at[k, place], near_buf.at[k, place], near_s.at[k], near_r.at[k], peer)

    def norm_middle(k):
        arrived(near_buf.at[k, pl.ds(1, 2 * tms - 1)], near_r.at[k])
        total = near_buf[k, 0]
        for i in range(1, 2 * tms):
            total = total + near_buf[k, i]
        place = r * groups + g
        wide_buf[k, place] = total
        for peer in wide_peers():
            send(wide_buf.at[k, place], wide_buf.at[k, place], wide_s.at[k], wide_r.at[k], peer)

    def norm_weight(k, weight, flag):
        arrived(wide_buf.at[k, pl.ds(1, groups * rws - 1)], wide_r.at[k])
        total = wide_buf[k, 0]
        for i in range(1, groups * rws):
            total = total + wide_buf[k, i]
        dx, dy = total[:, 0:scen], total[:, scen : 2 * scen]
        candidate = jnp.sqrt((dy + 1e-06) / (dx + 1e-06))
        return jnp.where(flag > 0.5, jnp.sqrt(weight * candidate), weight)

    for copy in small:
        copy.wait()
    eta, flag = plan(0)
    count = count + 1.0
    ybuf[0] = jnp.clip(-column(eta, 0, scen) * costs[0], 0.0, costs[1])
    left0 = stacked(ybuf[0])
    for i in range(rows // blk):
        loads[i].wait()
        part = pl.ds(i * blk, blk)
        for j in range(cols // blk):
            across = pl.ds(j * blk, blk)
            high, low = halves(kf[part, across] * bmap[i, j].astype(jnp.float32))
            kh[part, across] = high
            kl[part, across] = low
        pq[0, :, part] = product(left0, kh[part, :], kl[part, :], NT)
        if i == 1:
            pl.semaphore_wait(barrier, len(peers))
            send(ybuf.at[0, :, pl.ds(edge, stor)], halo.at[0], pair_sem.at[0], pair_sem.at[1], at(tm=rem(t + 1, tms)))
            send(costs, far, pair_sem.at[2], pair_sem.at[3], at(tm=o))
            pl.semaphore_signal(hello, inc=1, device_id=at(tm=ahead), device_id_type=MESH)
    loads[-1].wait()
    high, low = halves(lf[...])
    lh[...] = high
    ll[...] = low
    arrived(halo.at[0], pair_sem.at[1])
    left0 = stacked(halo[0])
    for some in (other_h, own_h):
        pq[0, :, some] = pq[0, :, some] + product(left0, lh[some, :], ll[some, :], NT)
        if some is other_h:
            send(pq.at[0, :, some], sib.at[0], sib_s.at[0], sib_r.at[0], sibling)
    sum_rows(0)
    arrived(far, pair_sem.at[3])
    pl.semaphore_wait(hello, 1)
    dx = primal_rest(0, count, flag)

    for k in range(ITERS):
        if k > 0:
            eta, flag = plan(k)
            count = count + 1.0
            apply_chunks(k, column(eta / weight, 0, scen))
            sum_rows(k)
            dx = primal_rest(k, count, flag)
            if k == ITERS - 1:
                primal_copy = pltpu.make_async_copy(zbuf, primal_out, out_sem.at[1])
                primal_copy.start()
        if k < ITERS - 1:
            dy = dual_step(k, weight, count, eta, flag)
            norm_start(k, dx, dy)
        else:
            viol, dual_part = dual_step(k, weight, count, eta, flag)
            fpart[0] = spread(viol / groups, 0) + spread(dual_part / groups, scen) + spread(dx, 2 * scen + own_r)
            send(fpart.at[0], fpart.at[1], pair_sem.at[4], pair_sem.at[5], at(tm=o))
        adjoint_own(k)
        arrived(wbuf.at[k, :, other_h], dual_r.at[k])
        dual_parts = stacked(wbuf[k, :, other_h])
        for j in range(len(CHUNKS)):
            adjoint_chunk(k, j, dual_parts)
            if j == 0:
                adjoint_side(k, dual_parts)
            if j == 2 and k < ITERS - 1:
                norm_middle(k)
        if k < ITERS - 1:
            adjoint_sums(k)
            weight = norm_weight(k, weight, flag)
            count = jnp.where(flag > 0.5, 0.0, count)

    k = ITERS - 1
    dual_copy = pltpu.make_async_copy(wbuf.at[k], dual_out, out_sem.at[0])
    dual_copy.start()
    arrived(fpart.at[1], pair_sem.at[5])
    bound = jnp.zeros((GROUP, 1), jnp.float32)
    for j in range(len(CHUNKS)):
        part = pl.ds(*CHUNKS[j])
        reduced = far[0, :, part] - receive_adjoint(k, j)
        bound = bound + jnp.sum(far[1, :, part] * jnp.minimum(reduced, 0.0), axis=1, keepdims=True)
    fsum[...] = fpart[1] + spread(bound, 3 * scen + own_r)
    for dr in far_first:
        for dc in (4, 3, 5, 2, 6, 1, 7, 0):
            place = at(tm=o, row=rem(r + dr, rws), col=rem(c + dc, cls))
            send(fsum, fall.at[r * cls + c], fall_sem.at[0], fall_sem.at[1], place)
    left(halo.at[0], pair_sem.at[0])
    left(costs, pair_sem.at[2])
    left(fpart.at[0], pair_sem.at[4])
    for k in range(ITERS):
        left(sib.at[k], sib_s.at[k])
        left(ysum.at[k, pl.ds(1, groups - 1)], y_s.at[k])
        left(sib.at[k], dual_s.at[k])
        left(side.at[k], side_s.at[k])
        left(pa.at[k], rsr_s.at[k])
        if k > 0:
            left(gbuf.at[k - 1], agr_s.at[k - 1])
            left(halo.at[k], halo_s.at[k])
        if k < ITERS - 1:
            left(near_buf.at[k, pl.ds(1, 2 * tms - 1)], near_s.at[k])
            left(wide_buf.at[k, pl.ds(1, groups * rws - 1)], wide_s.at[k])
    left(fall, fall_sem.at[0])
    dual_copy.wait()
    primal_copy.wait()
    arrived(fall, fall_sem.at[1])
    total = fall[0]
    for i in range(1, rws * cls):
        total = total + fall[i]
    con_total, var_total = float(rows * rws), float(cols * cls)
    parts = [total[:, i * scen : (i + 1) * scen] for i in range(4)]
    kkt_out[0, 0:1, :] = jnp.sqrt(parts[0] / con_total + 1e-06)
    kkt_out[0, 1:2, :] = parts[2] / var_total
    kkt_out[0, 2:3, :] = (parts[1] + parts[3]) / var_total


def on_device(matrix_tiles, block_map, link_tiles, demand, objective, upper_bound, restart_flag, step_index):
    rows, cols = matrix_tiles.shape
    stor = link_tiles.shape[1]
    scen = demand.shape[0]
    tms, rws, cls = lax.axis_size("tm"), lax.axis_size("row"), lax.axis_size("col")
    half = rows // 2
    groups = scen // GROUP
    f32, bf16 = jnp.float32, jnp.bfloat16
    vmem = pl.BlockSpec(memory_space=pltpu.VMEM)
    hbm = pl.BlockSpec(memory_space=pltpu.HBM)
    V = pltpu.VMEM
    D = pltpu.SemaphoreType.DMA
    n = ITERS
    scratch = [
        pltpu.SMEM(block_map.shape, jnp.int32), V(restart_flag.shape, jnp.int32), V(step_index.shape, jnp.int32),
        V((scen, half), f32), V((2, 1, cols), f32), V((2, 1, cols), f32),
        V((rows, cols), f32), V((rows, stor), f32),
        V((rows, cols), bf16), V((rows, cols), bf16), V((rows, stor), bf16), V((rows, stor), bf16),
        V((n, scen, cols), f32), V((n - 1, GROUP, cols), f32), V((n - 1, scen, cols), f32), V((n, scen, stor), f32), V((n, scen, rows), f32),
        V((n, scen, half), f32), V((n, groups, scen, half), f32),
        V((n, scen, rows), f32), V((n, scen, cols), f32), V((n, scen, stor), f32),
        V((n, rws, GROUP, cols), f32), V((n, rws, GROUP, stor), f32), V((scen, cols), f32),
        V((scen, cols), f32), V((scen, cols), f32), V((GROUP, cols), f32),
        V((scen, half), f32), V((scen, half), f32), V((scen, half), f32), V((scen, half), f32), V((scen, half), f32),
        V((n - 1, 2 * tms, 1, LANES), f32), V((n - 1, groups * rws, 1, LANES), f32),
        V((2, 1, LANES), f32), V((1, LANES), f32), V((rws * cls, 1, LANES), f32),
        D((block_map.shape[0] + 1,)), D((6,)), D((2,)), D((6,)), pltpu.SemaphoreType.REGULAR,
        D((n,)), D((n,)), D((n,)), D((n,)), D((n,)), D((n,)), D((n,)), D((n,)),
        D((n,)), D((n,)), D((n,)), D((n, len(CHUNKS))), D((n - 1,)), D((n - 1, len(CHUNKS))),
        D((n - 1,)), D((n - 1,)), D((n - 1,)), D((n - 1,)), D((2,)),
    ]
    return pl.pallas_call(
        functools.partial(kernel, (tms, rws, cls)),
        out_shape=(
            jax.ShapeDtypeStruct((scen, cols), f32),
            jax.ShapeDtypeStruct((scen, rows), f32),
            jax.ShapeDtypeStruct((1, 3, scen), f32),
        ),
        in_specs=[hbm] * 8,
        out_specs=(hbm, hbm, vmem),
        scratch_shapes=scratch,
        compiler_params=pltpu.CompilerParams(
            collective_id=0, has_side_effects=True, vmem_limit_bytes=48 << 20
        ),
        name="pdhg",
    )(*(
        pltpu.with_memory_space_constraint(x, pltpu.HBM)
        for x in (
            matrix_tiles, block_map, link_tiles, demand, objective.reshape(1, cols), upper_bound.reshape(1, cols),
            restart_flag, step_index,
        )
    ))


def solution(mesh):
    in_specs = (
        P(("tm", "row"), "col"),
        P(("tm", "row"), "col"),
        P(("tm", "row"), "col"),
        P(None, ("tm", "row")),
        P(("tm", "col")),
        P(("tm", "col")),
        P(),
        P(),
    )
    out_specs = (P(None, ("tm", "col")), P(None, ("tm", "row")), P("tm", None, None))
    return jax.shard_map(
        on_device, mesh=mesh, in_specs=in_specs, out_specs=out_specs, check_vma=False
    )
```

```python
import functools

import jax
import jax.numpy as jnp
from jax import lax
from jax.experimental import pallas as pl
from jax.experimental.pallas import tpu as pltpu
from jax.sharding import PartitionSpec as P

ITERS = 3
CHUNKS = ((0, 256), (1792, 256), (256, 512), (768, 512), (1280, 512))
LANES = 128
GROUP = 8
MESH = pl.DeviceIdType.MESH
NN = (((1,), (0,)), ((), ()))
NT = (((1,), (1,)), ((), ()))


def halves(x):
    high = x.astype(jnp.bfloat16)
    return high, (x - high.astype(jnp.float32)).astype(jnp.bfloat16)


def dot(a, b, dims):
    return lax.dot_general(a, b, dims, preferred_element_type=jnp.float32)


def product(left, high, low, dims):
    rows = left.shape[0] // 2
    both = dot(left, high, dims)
    return both[:rows] + (both[rows:] + dot(left[:rows], low, dims))


def stacked(x):
    return jnp.concatenate(halves(x), axis=0)


def column(row, start, size):
    shape = (size, row.shape[1])
    lane = lax.broadcasted_iota(jnp.int32, shape, 1)
    sub = lax.broadcasted_iota(jnp.int32, shape, 0)
    return jnp.sum(jnp.where(lane == sub + start, row, 0.0), axis=1, keepdims=True)


def spread(col, start):
    shape = (col.shape[0], LANES)
    lane = lax.broadcasted_iota(jnp.int32, shape, 1)
    sub = lax.broadcasted_iota(jnp.int32, shape, 0)
    return jnp.sum(jnp.where(lane == sub + start, col, 0.0), axis=0, keepdims=True)


def kernel(
    sizes,
    mat, bmap_in, link, dem_in, obj_in, ub_in, flags_in, steps_in,
    primal_out, dual_out, kkt_out,
    bmap, flags, steps, dem, costs, far,
    kf, lf, kh, kl, lh, ll,
    ybuf, gsum, gbuf, halo, pq, sib, ysum, wbuf, pa, side, ab, sb, zbuf,
    xs, xavg, xanc, ds, davg, danc, qx, qavg,
    near_buf, wide_buf, fpart, fsum, fall,
    load_sem, small_sem, out_sem, pair_sem, hello,
    halo_s, halo_r, sib_s, sib_r, y_s, y_r, dual_s, dual_r,
    side_s, side_r, rsr_s, rsr_r, agr_s, agr_r,
    near_s, near_r, wide_s, wide_r, fall_sem,
):
    tms, rws, cls = sizes
    rows, cols = kf.shape
    stor = lf.shape[1]
    edge = cols - stor
    scen = ybuf.shape[1]
    half = rows // 2
    groups = scen // GROUP
    blk = rows // bmap.shape[0]
    t, r, c = lax.axis_index("tm"), lax.axis_index("row"), lax.axis_index("col")
    g, h = lax.div(c, 2), lax.rem(c, 2)
    o = lax.rem(t + tms // 2, tms)
    own_r = pl.multiple_of(r * GROUP, GROUP)
    own_h = pl.ds(pl.multiple_of(h * half, half), half)
    other_h = pl.ds(pl.multiple_of((1 - h) * half, half), half)
    near_first = (0, 1, 3, 2)
    far_first = near_first[::-1]
    final = len(CHUNKS) - 1

    def rem(a, n):
        return lax.rem(a, n)

    def at(tm=None, row=None, col=None):
        return {"tm": t if tm is None else tm, "row": r if row is None else row, "col": c if col is None else col}

    def descriptor(src, dst, ssem, rsem, where):
        return pltpu.make_async_remote_copy(
            src_ref=src, dst_ref=dst, send_sem=ssem, recv_sem=rsem, device_id=where, device_id_type=MESH
        )

    def send(src, dst, ssem, rsem, where):
        descriptor(src, dst, ssem, rsem, where).start()

    def arrived(whole, sem):
        descriptor(whole, whole, sem, sem, at()).wait_recv()

    def left(whole, sem):
        descriptor(whole, whole, sem, sem, at()).wait_send()

    small = [
        pltpu.make_async_copy(src, dst, small_sem.at[i])
        for i, (src, dst) in enumerate(
            (
                (steps_in, steps), (obj_in, costs.at[0]), (ub_in, costs.at[1]), (bmap_in, bmap), (flags_in, flags),
                (dem_in.at[:, own_h], dem),
            )
        )
    ]
    loads = []
    for i in range(rows // blk):
        part = pl.ds(i * blk, blk)
        loads.append(pltpu.make_async_copy(mat.at[part], kf.at[part], load_sem.at[i]))
    loads.append(pltpu.make_async_copy(link, lf, load_sem.at[rows // blk]))
    for copy in small + loads:
        copy.start()

    def near_peers():
        for dt in range(tms):
            for f in range(2):
                if dt or f:
                    yield at(tm=rem(t + dt, tms), col=g * 2 + (1 - h if f else h))

    def wide_peers():
        for dr in (2, 1, 3, 0):
            for dg in range(groups):
                if dr or dg:
                    yield at(row=rem(r + dr, rws), col=rem(g + dg, groups) * 2 + h)

    behind, ahead = rem(o + tms - 1, tms), rem(o + 1, tms)
    barrier = pltpu.get_barrier_semaphore()
    peers = [at(row=rem(r + d, rws)) for d in (2, 1, 3)]
    peers += [at(tm=rem(t + d, tms)) for d in range(1, tms)]
    peers += [at(col=rem(c + d, cls)) for d in range(1, cls)]
    for peer in peers:
        pl.semaphore_signal(barrier, inc=1, device_id=peer, device_id_type=MESH)

    weight = jnp.ones((1, scen), jnp.float32)
    count = jnp.zeros((1, scen), jnp.float32)

    def plan(k):
        eta = 0.15 * (1.0 + steps[k : k + 1, :].astype(jnp.float32))
        flag = flags[k : k + 1, :].astype(jnp.float32)
        return eta, flag

    sibling = at(col=g * 2 + 1 - h)

    def sum_rows(k):
        arrived(sib.at[k], sib_r.at[k])
        ysum[k, g] = pq[k, :, own_h] + sib[k]
        for dg in (2, 1, 3):
            send(ysum.at[k, g], ysum.at[k, g], y_s.at[0], y_r.at[k], at(col=rem(g + dg, groups) * 2 + h))

    def dual_step(k, weight, count, eta, flag):
        sigma = column(eta * weight, 0, scen)
        cnt = column(count, 0, scen)
        flg = column(flag, 0, scen) > 0.5
        arrived(ysum.at[k, pl.ds(1, groups - 1)], y_r.at[k])
        q = ysum[k, 0]
        for i in range(1, groups):
            q = q + ysum[k, i]
        mine = dem[...]
        if k == 0:
            nxt = jnp.maximum(sigma * (mine - 2.0 * q), 0.0)
            avg, qa = nxt, q
            dual = nxt
            anchor = jnp.zeros_like(nxt)
        else:
            nxt = jnp.maximum(ds[...] + sigma * (mine - (2.0 * q - qx[...])), 0.0)
            avg = davg[...] + (nxt - davg[...]) / cnt
            qa = qavg[...] + (q - qavg[...]) / cnt
            dual = jnp.where(flg, avg, nxt)
            anchor = danc[...]
        ds[...] = dual
        wbuf[k, :, own_h] = dual
        send(wbuf.at[k, :, own_h], wbuf.at[k, :, own_h], dual_s.at[0], dual_r.at[k], sibling)
        davg[...] = avg
        qavg[...] = qa
        q_now = jnp.where(flg, qa, q)
        qx[...] = q_now
        dist = jnp.sum(jnp.square(avg - anchor), axis=1, keepdims=True)
        danc[...] = jnp.where(flg, avg, anchor)
        if k < ITERS - 1:
            return dist
        violation = jnp.sum(jnp.square(jnp.maximum(mine - q_now, 0.0)), axis=1, keepdims=True)
        return violation, jnp.sum(mine * dual, axis=1, keepdims=True)

    def adjoint_own(k):
        parts = stacked(wbuf[k, :, own_h])
        for first, size in CHUNKS:
            part = pl.ds(first, size)
            pa[k, :, part] = product(parts, kh[own_h, part], kl[own_h, part], NN)
        side[k] = product(parts, lh[own_h, :], ll[own_h, :], NN)

    def adjoint_side(k, left):
        side[k] = side[k] + product(left, lh[other_h, :], ll[other_h, :], NN)
        for d in range(rws):
            to_r = rem(r + d, rws)
            src = side.at[k, pl.ds(pl.multiple_of(to_r * GROUP, GROUP), GROUP)]
            send(src, sb.at[k, d], side_s.at[0], side_r.at[k], at(tm=behind, row=to_r))

    def adjoint_chunk(k, j, left):
        part = pl.ds(*CHUNKS[j])
        pa[k, :, part] = pa[k, :, part] + product(left, kh[other_h, part], kl[other_h, part], NN)
        for d in far_first:
            to_r = rem(r + d, rws)
            src = pa.at[k, pl.ds(pl.multiple_of(to_r * GROUP, GROUP), GROUP), part]
            send(src, ab.at[k, d, :, part], rsr_s.at[0], rsr_r.at[k, j], at(tm=o, row=to_r))

    def receive_adjoint(k, j):
        part = pl.ds(*CHUNKS[j])
        arrived(ab.at[k, :, :, part], rsr_r.at[k, j])
        total = (ab[k, 0, :, part] + ab[k, 1, :, part]) + (ab[k, 2, :, part] + ab[k, 3, :, part])
        if CHUNKS[j][0] == edge:
            arrived(sb.at[k], side_r.at[k])
            extra = (sb[k, 0] + sb[k, 1]) + (sb[k, 2] + sb[k, 3])
            total = total + extra
        return total

    def adjoint_sums(k):
        for j in range(len(CHUNKS)):
            part = pl.ds(*CHUNKS[j])
            gsum[k, :, part] = receive_adjoint(k, j)
            for d in far_first:
                send(
                    gsum.at[k, :, part], gbuf.at[k, pl.ds(own_r, GROUP), part],
                    agr_s.at[0], agr_r.at[k, j], at(tm=o, row=rem(r + d, rws)),
                )

    def primal_rest(k, count, flag):
        cnt = column(count, 0, scen)
        flg = column(flag, 0, scen) > 0.5
        mine = pl.ds(own_r, GROUP)
        for first, size in CHUNKS:
            part = pl.ds(first, size)
            nxt = ybuf[k, :, part]
            avg = nxt if k == 0 else xavg[:, part] + (nxt - xavg[:, part]) / cnt
            xavg[:, part] = avg
            now = jnp.where(flg, avg, nxt)
            if k < ITERS - 1:
                xs[:, part] = now
            else:
                zbuf[:, part] = now
        if k == ITERS - 1:
            return jnp.sum(costs[0] * zbuf[mine, :], axis=1, keepdims=True)
        avg = xavg[mine, :]
        anchor = jnp.zeros_like(avg) if k == 0 else xanc[...]
        xanc[...] = jnp.where(column(flag, own_r, GROUP) > 0.5, avg, anchor)
        return jnp.sum(jnp.square(avg - anchor), axis=1, keepdims=True)

    def apply_chunks(k, tau):
        for j in range(len(CHUNKS)):
            part = pl.ds(*CHUNKS[j])
            arrived(gbuf.at[k - 1, :, part], agr_r.at[k - 1, j])
            reduced = costs[0, :, part] - gbuf[k - 1, :, part]
            nxt = jnp.clip(xs[:, part] - tau * reduced, 0.0, costs[1, :, part])
            ybuf[k, :, part] = nxt
            left = stacked(nxt)
            if CHUNKS[j][0] == edge:
                send(ybuf.at[k, :, part], halo.at[k], halo_s.at[0], halo_r.at[k], at(tm=rem(t + 1, tms)))
            if j != final:
                term = product(left, kh[:, part], kl[:, part], NT)
                if j == final - 1:
                    arrived(halo.at[k], halo_r.at[k])
                    term = term + product(stacked(halo[k]), lh[...], ll[...], NT)
                pq[k] = term if j == 0 else pq[k] + term
            else:
                for some in (other_h, own_h):
                    pq[k, :, some] = pq[k, :, some] + product(left, kh[some, part], kl[some, part], NT)
                    if some is other_h:
                        send(pq.at[k, :, some], sib.at[k], sib_s.at[0], sib_r.at[k], sibling)

    def norm_start(k, dx, dy):
        place = t * 2 + h
        near_buf[k, place] = spread(dx, own_r) + spread(dy / groups, scen)
        for peer in near_peers():
            send(near_buf.at[k, place], near_buf.at[k, place], near_s.at[0], near_r.at[k], peer)

    def norm_middle(k):
        arrived(near_buf.at[k, pl.ds(1, 2 * tms - 1)], near_r.at[k])
        total = near_buf[k, 0]
        for i in range(1, 2 * tms):
            total = total + near_buf[k, i]
        place = r * groups + g
        wide_buf[k, place] = total
        for peer in wide_peers():
            send(wide_buf.at[k, place], wide_buf.at[k, place], wide_s.at[0], wide_r.at[k], peer)

    def norm_weight(k, weight, flag):
        arrived(wide_buf.at[k, pl.ds(1, groups * rws - 1)], wide_r.at[k])
        total = wide_buf[k, 0]
        for i in range(1, groups * rws):
            total = total + wide_buf[k, i]
        dx, dy = total[:, 0:scen], total[:, scen : 2 * scen]
        candidate = jnp.sqrt((dy + 1e-06) / (dx + 1e-06))
        return jnp.where(flag > 0.5, jnp.sqrt(weight * candidate), weight)

    for copy in small:
        copy.wait()
    eta, flag = plan(0)
    count = count + 1.0
    ybuf[0] = jnp.clip(-column(eta, 0, scen) * costs[0], 0.0, costs[1])
    left0 = stacked(ybuf[0])
    for i in range(rows // blk):
        loads[i].wait()
        part = pl.ds(i * blk, blk)
        for j in range(cols // blk):
            across = pl.ds(j * blk, blk)
            high, low = halves(kf[part, across] * bmap[i, j].astype(jnp.float32))
            kh[part, across] = high
            kl[part, across] = low
        pq[0, :, part] = product(left0, kh[part, :], kl[part, :], NT)
        if i == 1:
            pl.semaphore_wait(barrier, len(peers))
            send(ybuf.at[0, :, pl.ds(edge, stor)], halo.at[0], pair_sem.at[0], pair_sem.at[1], at(tm=rem(t + 1, tms)))
            send(costs, far, pair_sem.at[2], pair_sem.at[3], at(tm=o))
            pl.semaphore_signal(hello, inc=1, device_id=at(tm=ahead), device_id_type=MESH)
    loads[-1].wait()
    high, low = halves(lf[...])
    lh[...] = high
    ll[...] = low
    arrived(halo.at[0], pair_sem.at[1])
    left0 = stacked(halo[0])
    for some in (other_h, own_h):
        pq[0, :, some] = pq[0, :, some] + product(left0, lh[some, :], ll[some, :], NT)
        if some is other_h:
            send(pq.at[0, :, some], sib.at[0], sib_s.at[0], sib_r.at[0], sibling)
    sum_rows(0)
    arrived(far, pair_sem.at[3])
    pl.semaphore_wait(hello, 1)
    dx = primal_rest(0, count, flag)

    for k in range(ITERS):
        if k > 0:
            eta, flag = plan(k)
            count = count + 1.0
            apply_chunks(k, column(eta / weight, 0, scen))
            sum_rows(k)
            dx = primal_rest(k, count, flag)
            if k == ITERS - 1:
                primal_copy = pltpu.make_async_copy(zbuf, primal_out, out_sem.at[1])
                primal_copy.start()
        if k < ITERS - 1:
            dy = dual_step(k, weight, count, eta, flag)
            norm_start(k, dx, dy)
        else:
            viol, dual_part = dual_step(k, weight, count, eta, flag)
            fpart[0] = spread(viol / groups, 0) + spread(dual_part / groups, scen) + spread(dx, 2 * scen + own_r)
            send(fpart.at[0], fpart.at[1], pair_sem.at[4], pair_sem.at[5], at(tm=o))
        adjoint_own(k)
        arrived(wbuf.at[k, :, other_h], dual_r.at[k])
        dual_parts = stacked(wbuf[k, :, other_h])
        for j in range(len(CHUNKS)):
            adjoint_chunk(k, j, dual_parts)
            if j == 0:
                adjoint_side(k, dual_parts)
            if j == 2 and k < ITERS - 1:
                norm_middle(k)
        if k < ITERS - 1:
            adjoint_sums(k)
            weight = norm_weight(k, weight, flag)
            count = jnp.where(flag > 0.5, 0.0, count)

    k = ITERS - 1
    dual_copy = pltpu.make_async_copy(wbuf.at[k], dual_out, out_sem.at[0])
    dual_copy.start()
    arrived(fpart.at[1], pair_sem.at[5])
    bound = jnp.zeros((GROUP, 1), jnp.float32)
    for j in range(len(CHUNKS)):
        part = pl.ds(*CHUNKS[j])
        reduced = far[0, :, part] - receive_adjoint(k, j)
        bound = bound + jnp.sum(far[1, :, part] * jnp.minimum(reduced, 0.0), axis=1, keepdims=True)
    fsum[...] = fpart[1] + spread(bound, 3 * scen + own_r)
    for dr in far_first:
        for dc in (4, 3, 5, 2, 6, 1, 7, 0):
            place = at(tm=o, row=rem(r + dr, rws), col=rem(c + dc, cls))
            send(fsum, fall.at[r * cls + c], fall_sem.at[0], fall_sem.at[1], place)
    left(halo.at[0], pair_sem.at[0])
    left(costs, pair_sem.at[2])
    left(fpart.at[0], pair_sem.at[4])
    left(sib, sib_s.at[0])
    left(ysum.at[:, pl.ds(1, groups - 1)], y_s.at[0])
    left(sib, dual_s.at[0])
    left(side, side_s.at[0])
    left(pa, rsr_s.at[0])
    left(gbuf, agr_s.at[0])
    left(halo.at[pl.ds(1, ITERS - 1)], halo_s.at[0])
    left(near_buf.at[:, pl.ds(1, 2 * tms - 1)], near_s.at[0])
    left(wide_buf.at[:, pl.ds(1, groups * rws - 1)], wide_s.at[0])
    left(fall, fall_sem.at[0])
    dual_copy.wait()
    primal_copy.wait()
    arrived(fall, fall_sem.at[1])
    total = fall[0]
    for i in range(1, rws * cls):
        total = total + fall[i]
    con_total, var_total = float(rows * rws), float(cols * cls)
    parts = [total[:, i * scen : (i + 1) * scen] for i in range(4)]
    kkt_out[0] = jnp.sqrt(parts[0] / con_total + 1e-06)
    kkt_out[1] = parts[2] / var_total
    kkt_out[2] = (parts[1] + parts[3]) / var_total


def on_device(matrix_tiles, block_map, link_tiles, demand, objective, upper_bound, restart_flag, step_index):
    rows, cols = matrix_tiles.shape
    stor = link_tiles.shape[1]
    scen = demand.shape[0]
    tms, rws, cls = lax.axis_size("tm"), lax.axis_size("row"), lax.axis_size("col")
    half = rows // 2
    groups = scen // GROUP
    f32, bf16 = jnp.float32, jnp.bfloat16
    vmem = pl.BlockSpec(memory_space=pltpu.VMEM)
    hbm = pl.BlockSpec(memory_space=pltpu.HBM)
    V = pltpu.VMEM
    D = pltpu.SemaphoreType.DMA
    n = ITERS
    scratch = [
        pltpu.SMEM(block_map.shape, jnp.int32), V(restart_flag.shape, jnp.int32), V(step_index.shape, jnp.int32),
        V((scen, half), f32), V((2, 1, cols), f32), V((2, 1, cols), f32),
        V((rows, cols), f32), V((rows, stor), f32),
        V((rows, cols), bf16), V((rows, cols), bf16), V((rows, stor), bf16), V((rows, stor), bf16),
        V((n, scen, cols), f32), V((n - 1, GROUP, cols), f32), V((n - 1, scen, cols), f32), V((n, scen, stor), f32), V((n, scen, rows), f32),
        V((n, scen, half), f32), V((n, groups, scen, half), f32),
        V((n, scen, rows), f32), V((n, scen, cols), f32), V((n, scen, stor), f32),
        V((n, rws, GROUP, cols), f32), V((n, rws, GROUP, stor), f32), V((scen, cols), f32),
        V((scen, cols), f32), V((scen, cols), f32), V((GROUP, cols), f32),
        V((scen, half), f32), V((scen, half), f32), V((scen, half), f32), V((scen, half), f32), V((scen, half), f32),
        V((n - 1, 2 * tms, 1, LANES), f32), V((n - 1, groups * rws, 1, LANES), f32),
        V((2, 1, LANES), f32), V((1, LANES), f32), V((rws * cls, 1, LANES), f32),
        D((block_map.shape[0] + 1,)), D((6,)), D((2,)), D((6,)), pltpu.SemaphoreType.REGULAR,
        D((1,)), D((n,)), D((1,)), D((n,)), D((1,)), D((n,)), D((1,)), D((n,)),
        D((1,)), D((n,)), D((1,)), D((n, len(CHUNKS))), D((1,)), D((n - 1, len(CHUNKS))),
        D((1,)), D((n - 1,)), D((1,)), D((n - 1,)), D((2,)),
    ]
    primal, dual, kkt = pl.pallas_call(
        functools.partial(kernel, (tms, rws, cls)),
        out_shape=(
            jax.ShapeDtypeStruct((scen, cols), f32),
            jax.ShapeDtypeStruct((scen, rows), f32),
            jax.ShapeDtypeStruct((3, 1, scen), f32),
        ),
        in_specs=[hbm] * 8,
        out_specs=(hbm, hbm, vmem),
        scratch_shapes=scratch,
        compiler_params=pltpu.CompilerParams(
            collective_id=0, has_side_effects=True, vmem_limit_bytes=48 << 20
        ),
        name="pdhg",
    )(*(
        pltpu.with_memory_space_constraint(x, pltpu.HBM)
        for x in (
            matrix_tiles, block_map, link_tiles, demand, objective.reshape(1, cols), upper_bound.reshape(1, cols),
            restart_flag, step_index,
        )
    ))
    return primal, dual, kkt.transpose(1, 0, 2)


def solution(mesh):
    in_specs = (
        P(("tm", "row"), "col"),
        P(("tm", "row"), "col"),
        P(("tm", "row"), "col"),
        P(None, ("tm", "row")),
        P(("tm", "col")),
        P(("tm", "col")),
        P(),
        P(),
    )
    out_specs = (P(None, ("tm", "col")), P(None, ("tm", "row")), P("tm", None, None))
    return jax.shard_map(
        on_device, mesh=mesh, in_specs=in_specs, out_specs=out_specs, check_vma=False
    )
```
